256 devices in a mesh: row: 16 (over z, core), col: 16 (over y, x).
Axes of the slice: x: 4, y: 4, z: 8, core: 2. Of those that a mesh axis runs over, the one named last changes fastest.
Arguments:
- source_embed: bfloat16 [32768, 256], P('row'), may hold values from -16 to 16
- target_embed: bfloat16 [32768, 256], P('col'), may hold values from -16 to 16
- source_logmass: float32 [32768], P('row'), may hold values from -6 to 6
- target_logmass: float32 [32768], P('col'), may hold values from -6 to 6
- tile_rows: int32 [16, 16, 128], P('row', 'col'), may hold values from 0 to 15, as said below
- tile_columns: int32 [16, 16, 128], P('row', 'col'), may hold values from 0 to 15, as said below
- tile_counts: int32 [16, 16], P('row', 'col'), may hold values from 16 to 128, as said below
- row_cotangent: float32 [32768], P('row'), may hold values from -6 to 6
- column_cotangent: float32 [32768], P('col'), may hold values from -6 to 6
Outputs:
- source_potential: float32 [32768], P('row')
- target_potential: float32 [32768], P('col')
- source_grad: float32 [32768, 256], P(('row', 'col'))
- target_grad: float32 [32768, 256], P(('col', 'row'))
The draws below stay inside these ranges and needn't reach their ends.
Inputs may be any that keep to these rules, and one draw needn't show every extreme that they name: `tile_rows`: the valid slots of one device name distinct tiles; its first 16 slots are the tiles (k, k) for k = 0 .. 15 in order; slots at or after the device's count hold 0. `tile_columns`: as tile_rows; slots at or after the device's count hold 0. `tile_counts`: some device has all 128 slots valid.
All inputs are finite; a program needn't handle non-finite values.
Results may differ from the reference program's by a relative error of at most 0.01.
Values sent between devices are 32-bit elements; how exact they have to be, the bound alone decides.
A program may use at most 128 MiB of HBM per device.

```python
import jax
import jax.numpy as jnp
from jax import lax

E = 256
TB = 128
CELLS_DEV = 2048
ITERS = 3
BLOCKS = 16
TILES = 128
N_SRC = 32768
N_TGT = 32768
N_ROW = 16
N_COL = 16


def target_rows_base(key):
    base_key = jax.random.fold_in(key, 101)
    normal_key, sign_key = jax.random.split(base_key)
    base_rows = jax.random.truncated_normal(normal_key, -4.0, 4.0, (N_TGT, E), jnp.float32) * 0.45
    signs = jnp.where(jax.random.bernoulli(sign_key, 0.5, (N_TGT, E)), 1.0, -1.0).astype(jnp.float32)
    chosen_rows = (jnp.arange(N_TGT) % TB == 5)[:, None]
    return jnp.where(chosen_rows, 2.0 * signs, base_rows)


def tile_lists(key):
    list_key = jax.random.fold_in(key, 55)
    count_key, full_key, perm_key = jax.random.split(list_key, 3)
    device_total = N_ROW * N_COL
    levels = jax.random.randint(count_key, (device_total,), 0, 9)
    counts = BLOCKS + levels * levels * (TILES - BLOCKS) // 64
    full_device = jax.random.randint(full_key, (), 0, device_total)
    counts = jnp.where(jnp.arange(device_total) == full_device, TILES, counts)
    off_total = BLOCKS * (BLOCKS - 1)
    perm_keys = jax.random.split(perm_key, device_total)
    perms = jax.vmap(lambda single: jax.random.permutation(single, off_total))(perm_keys)
    chosen = perms[:, :TILES - BLOCKS]
    off_rows = chosen // (BLOCKS - 1)
    raw_cols = chosen % (BLOCKS - 1)
    off_cols = raw_cols + (raw_cols >= off_rows).astype(jnp.int32)
    diagonal = jnp.broadcast_to(jnp.arange(BLOCKS, dtype=jnp.int32), (device_total, BLOCKS))
    rows = jnp.concatenate([diagonal, off_rows.astype(jnp.int32)], axis=1)
    cols = jnp.concatenate([diagonal, off_cols.astype(jnp.int32)], axis=1)
    live_slot = jnp.arange(TILES)[None, :] < counts[:, None]
    rows = jnp.where(live_slot, rows, 0).astype(jnp.int32)
    cols = jnp.where(live_slot, cols, 0).astype(jnp.int32)
    shape = (N_ROW, N_COL, TILES)
    return (rows.reshape(shape), cols.reshape(shape), counts.astype(jnp.int32).reshape(N_ROW, N_COL))


def draw_tile_rows(key, part):
    rows, cols, counts = tile_lists(key)
    return rows


def draw_tile_columns(key, part):
    rows, cols, counts = tile_lists(key)
    return cols


def draw_tile_counts(key, part):
    rows, cols, counts = tile_lists(key)
    return counts


def draw_target_embed(key, part):
    base_rows = target_rows_base(key)
    return base_rows.astype(jnp.bfloat16)


def draw_source_embed(key, part):
    target_rows = target_rows_base(key)
    key = jax.random.fold_in(key, 9)
    noise_key = jax.random.fold_in(key, 0)
    stretch_key = jax.random.fold_in(key, 2)
    base_rows = jax.random.truncated_normal(noise_key, -4.0, 4.0, (N_SRC, E), jnp.float32) * 0.45
    row_index = jnp.arange(N_SRC)
    partner = row_index % CELLS_DEV // TB * TB + 5
    levels = jax.random.randint(stretch_key, (N_SRC,), 0, 3)
    stretch = jnp.where(levels == 0, 55.0, jnp.where(levels == 1, 85.0, 125.0)) / (2.0 * E)
    aligned = target_rows[partner] * stretch[:, None]
    chosen_rows = (row_index % TB == 0)[:, None]
    base_rows = jnp.where(chosen_rows, aligned, base_rows)
    return base_rows.astype(jnp.bfloat16)


def level_of(stream_key, dims, pieces, least, high):
    def one(dim, shards_of):
        heights = jax.random.uniform(jax.random.fold_in(jax.random.fold_in(stream_key, 6), dim), (shards_of,), jnp.float32, least / len(pieces), high / len(pieces))
        return jnp.repeat(jnp.exp(heights), dims[dim] // shards_of).reshape((-1,) + (1,) * (len(dims) - dim - 1))

    gain = one(*pieces[0])
    for cut in pieces[1:]:
        gain = gain * one(*cut)
    return gain


def scatter_about(stream_key, shape, spread, bound, pieces=(), kind=jnp.bfloat16):
    drawn = jax.random.normal(stream_key, shape, jnp.float32) * spread
    if len(pieces) > 0:
        drawn = level_of(stream_key, shape, pieces, -0.22, 0.18) * drawn
    return jnp.clip(drawn, min=-bound, max=bound).astype(kind)


def setup_inputs(seed: int = 0) -> dict:
    seeds = jax.random.split(jax.random.key(seed), 10)
    source_embed = draw_source_embed(jax.random.fold_in(seeds[9], 71), 0)
    target_embed = draw_target_embed(jax.random.fold_in(seeds[9], 71), 0)
    source_logmass = scatter_about(seeds[2], (N_SRC,), 1.0, 6.0, ((0, 16),), jnp.float32)
    target_logmass = scatter_about(seeds[3], (N_TGT,), 1.0, 6.0, ((0, 16),), jnp.float32)
    tile_rows = draw_tile_rows(jax.random.fold_in(seeds[9], 71), 0)
    tile_columns = draw_tile_columns(jax.random.fold_in(seeds[9], 71), 0)
    tile_counts = draw_tile_counts(jax.random.fold_in(seeds[9], 71), 0)
    row_cotangent = scatter_about(seeds[7], (N_SRC,), 1.0, 6.0, ((0, 16),), jnp.float32)
    column_cotangent = scatter_about(seeds[8], (N_TGT,), 1.0, 6.0, ((0, 16),), jnp.float32)
    return {"source_embed": source_embed, "target_embed": target_embed, "source_logmass": source_logmass, "target_logmass": target_logmass, "tile_rows": tile_rows, "tile_columns": tile_columns, "tile_counts": tile_counts, "row_cotangent": row_cotangent, "column_cotangent": column_cotangent}


floor_value = -1.0e30


def device_view(device, source_embed, target_embed, tile_rows, tile_columns, tile_counts):
    row_dev = device // N_COL
    col_dev = device % N_COL
    src_local = lax.dynamic_slice_in_dim(source_embed, row_dev * CELLS_DEV, CELLS_DEV, 0).reshape(BLOCKS, TB, E)
    tgt_local = lax.dynamic_slice_in_dim(target_embed, col_dev * CELLS_DEV, CELLS_DEV, 0).reshape(BLOCKS, TB, E)
    row_ids = tile_rows[row_dev, col_dev]
    col_ids = tile_columns[row_dev, col_dev]
    live_slot = jnp.arange(TILES, dtype=jnp.int32) < tile_counts[row_dev, col_dev]
    src_tiles = src_local[row_ids].astype(jnp.float32)
    tgt_tiles = tgt_local[col_ids].astype(jnp.float32)
    scores = jnp.einsum("tpe,tqe->tpq", src_tiles, tgt_tiles, precision=lax.Precision.HIGHEST)
    return row_dev, col_dev, row_ids, col_ids, live_slot, scores, src_tiles, tgt_tiles


def local_blocks(vector, owner):
    return lax.dynamic_slice_in_dim(vector, owner * CELLS_DEV, CELLS_DEV, 0).reshape(BLOCKS, TB)


def partial_lse(shifted, own_ids, live_slot):
    tile_max = jnp.where(live_slot[:, None], jnp.max(shifted, axis=2), floor_value)
    partial_max = jnp.full((BLOCKS, TB), floor_value, jnp.float32).at[own_ids].max(tile_max)
    terms = jnp.sum(jnp.exp(shifted - partial_max[own_ids][:, :, None]), axis=2)
    terms = jnp.where(live_slot[:, None], terms, 0.0)
    partial_sum = jnp.zeros((BLOCKS, TB), jnp.float32).at[own_ids].add(terms)
    return partial_max.reshape(-1), partial_sum.reshape(-1)


def combine_lse(partial_max, partial_sum, axis):
    largest = jnp.max(partial_max, axis=axis, keepdims=True)
    summed = jnp.sum(partial_sum * jnp.exp(partial_max - largest), axis=axis)
    return (jnp.squeeze(largest, axis) + jnp.log(summed)).reshape(-1)


def reference(source_embed, target_embed, source_logmass, target_logmass, tile_rows, tile_columns, tile_counts, row_cotangent, column_cotangent):
    devices = jnp.arange(N_ROW * N_COL, dtype=jnp.int32)

    def view(device):
        return device_view(device, source_embed, target_embed, tile_rows, tile_columns, tile_counts)

    def row_partials(col_pot):
        def one(device):
            row_dev, col_dev, row_ids, col_ids, live_slot, scores, src_tiles, tgt_tiles = view(device)
            shifted = scores + local_blocks(col_pot, col_dev)[col_ids][:, None, :]
            return partial_lse(shifted, row_ids, live_slot)
        partial_max, partial_sum = lax.map(one, devices)
        shape = (N_ROW, N_COL, CELLS_DEV)
        return combine_lse(partial_max.reshape(shape), partial_sum.reshape(shape), 1)

    def col_partials(row_pot):
        def one(device):
            row_dev, col_dev, row_ids, col_ids, live_slot, scores, src_tiles, tgt_tiles = view(device)
            shifted = jnp.swapaxes(scores, 1, 2) + local_blocks(row_pot, row_dev)[row_ids][:, None, :]
            return partial_lse(shifted, col_ids, live_slot)
        partial_max, partial_sum = lax.map(one, devices)
        shape = (N_ROW, N_COL, CELLS_DEV)
        return combine_lse(partial_max.reshape(shape), partial_sum.reshape(shape), 0)

    col_pot = jnp.zeros((N_TGT,), jnp.float32)
    row_pots = []
    col_pots = [col_pot]
    for iteration in range(ITERS):
        row_pot = source_logmass - row_partials(col_pot)
        col_pot = target_logmass - col_partials(row_pot)
        row_pots.append(row_pot)
        col_pots.append(col_pot)

    def col_plan(device, iteration):
        row_dev, col_dev, row_ids, col_ids, live_slot, scores, src_tiles, tgt_tiles = view(device)
        row_add = local_blocks(row_pots[iteration], row_dev)[row_ids]
        col_add = local_blocks(col_pots[iteration + 1] - target_logmass, col_dev)[col_ids]
        plan = jnp.exp(scores + row_add[:, :, None] + col_add[:, None, :])
        return jnp.where(live_slot[:, None, None], plan, 0.0)

    def row_plan(device, iteration):
        row_dev, col_dev, row_ids, col_ids, live_slot, scores, src_tiles, tgt_tiles = view(device)
        row_add = local_blocks(row_pots[iteration] - source_logmass, row_dev)[row_ids]
        col_add = local_blocks(col_pots[iteration], col_dev)[col_ids]
        plan = jnp.exp(scores + row_add[:, :, None] + col_add[:, None, :])
        return jnp.where(live_slot[:, None, None], plan, 0.0)

    row_adjs = [None] * ITERS
    col_adjs = [None] * ITERS
    col_adj = column_cotangent
    for iteration in reversed(range(ITERS)):
        col_adjs[iteration] = col_adj

        def row_side(device):
            row_dev, col_dev, row_ids, col_ids, live_slot, scores, src_tiles, tgt_tiles = view(device)
            plan = col_plan(device, iteration)
            weights = local_blocks(col_adj, col_dev)[col_ids]
            partial_value = jnp.sum(plan * weights[:, None, :], axis=2)
            return jnp.zeros((BLOCKS, TB), jnp.float32).at[row_ids].add(partial_value).reshape(-1)

        summed = jnp.sum(lax.map(row_side, devices).reshape(N_ROW, N_COL, CELLS_DEV), axis=1).reshape(-1)
        row_adj = -summed
        if iteration == ITERS - 1:
            row_adj = row_cotangent - summed
        row_adjs[iteration] = row_adj
        if iteration > 0:
            def col_side(device):
                row_dev, col_dev, row_ids, col_ids, live_slot, scores, src_tiles, tgt_tiles = view(device)
                plan = row_plan(device, iteration)
                weights = local_blocks(row_adj, row_dev)[row_ids]
                partial_value = jnp.sum(plan * weights[:, :, None], axis=1)
                return jnp.zeros((BLOCKS, TB), jnp.float32).at[col_ids].add(partial_value).reshape(-1)

            summed_cols = jnp.sum(lax.map(col_side, devices).reshape(N_ROW, N_COL, CELLS_DEV), axis=0).reshape(-1)
            col_adj = -summed_cols

    def grad_step(state, device):
        grad_src, grad_tgt = state
        row_dev, col_dev, row_ids, col_ids, live_slot, scores, src_tiles, tgt_tiles = view(device)
        score_cot = jnp.zeros((TILES, TB, TB), jnp.float32)
        for iteration in reversed(range(ITERS)):
            col_w = local_blocks(col_adjs[iteration], col_dev)[col_ids]
            row_w = local_blocks(row_adjs[iteration], row_dev)[row_ids]
            score_cot = score_cot - col_plan(device, iteration) * col_w[:, None, :]
            score_cot = score_cot - row_plan(device, iteration) * row_w[:, :, None]
        rounded = lax.optimization_barrier(score_cot.astype(jnp.bfloat16))
        widened = rounded.astype(jnp.float32)
        row_terms = jnp.einsum("tpq,tqe->tpe", widened, tgt_tiles, precision=lax.Precision.HIGHEST)
        col_terms = jnp.einsum("tpq,tpe->tqe", widened, src_tiles, precision=lax.Precision.HIGHEST)
        src_part = jnp.zeros((BLOCKS, TB, E), jnp.float32).at[row_ids].add(row_terms).reshape(CELLS_DEV, E)
        tgt_part = jnp.zeros((BLOCKS, TB, E), jnp.float32).at[col_ids].add(col_terms).reshape(CELLS_DEV, E)
        src_start = row_dev * CELLS_DEV
        tgt_start = col_dev * CELLS_DEV
        grad_src = lax.dynamic_update_slice_in_dim(grad_src, lax.dynamic_slice_in_dim(grad_src, src_start, CELLS_DEV, 0) + src_part, src_start, 0)
        grad_tgt = lax.dynamic_update_slice_in_dim(grad_tgt, lax.dynamic_slice_in_dim(grad_tgt, tgt_start, CELLS_DEV, 0) + tgt_part, tgt_start, 0)
        return (grad_src, grad_tgt), None

    start_state = (jnp.zeros((N_SRC, E), jnp.float32), jnp.zeros((N_TGT, E), jnp.float32))
    (source_grad, target_grad), unused = lax.scan(grad_step, start_state, devices)
    return row_pots[-1], col_pots[-1], source_grad, target_grad
```

```python
import jax
import jax.numpy as jnp
from jax import lax
from jax.experimental import pallas as pl
from jax.experimental.pallas import tpu as pltpu
from jax.sharding import PartitionSpec as P

MESH = pl.DeviceIdType.MESH
TB = 128
NB = 16
CELLS = NB * TB
E = 256
ROUNDS = 11
MASKED = -1e30
F32 = jnp.float32
BF16 = jnp.bfloat16
SHRINK = 2.0**-40
GROW = 2.0**40


def nt_dot(x, y):
    return lax.dot_general(x, y, (((1,), (1,)), ((), ())), preferred_element_type=F32)


def tn_dot(x, y):
    return lax.dot_general(x, y, (((0,), (0,)), ((), ())), preferred_element_type=F32)


def block(index, size=TB):
    return pl.ds(pl.multiple_of(index * size, size), size)


def kernel(
    src, tgt, a_ref, b_ref, rows_ref, cols_ref, count_ref, rc_ref, cc_ref,
    f_out, g_out, gs_out, gt_out,
    q, w, part, land, wide, wide2, bias, vec, vec_w, srct, xs, ys, xb, yb,
    gs_send, gs_land, gt_part, gt_sib, gt_send, gt_land,
    ar_send, ar_recv, gs_ssem, gs_rsem, sib_ssem, sib_rsem, gt_ssem, gt_rsem,
):
    row_me = lax.axis_index("row")
    col_me = lax.axis_index("col")
    z_me = row_me // 2
    core = row_me % 2
    y_me = col_me // 4
    x_me = col_me % 4

    barrier = pltpu.get_barrier_semaphore()

    @pl.loop(1, NB)
    def _(k):
        pl.semaphore_signal(
            barrier, inc=1, device_id={"row": lax.rem(row_me + k, NB)}, device_id_type=MESH
        )
        pl.semaphore_signal(
            barrier, inc=1, device_id={"col": lax.rem(col_me + k, NB)}, device_id_type=MESH
        )

    eye = lax.broadcasted_iota(jnp.int32, (TB, TB), 0) == lax.broadcasted_iota(
        jnp.int32, (TB, TB), 1
    )

    def to_row(column):
        return jnp.sum(jnp.where(eye, column, 0.0), axis=0, keepdims=True)

    def to_column(row):
        return jnp.sum(jnp.where(eye, row, 0.0), axis=1, keepdims=True)

    def widen(value):
        vec[...] = value
        for rb in range(NB):
            wide[rb * TB : (rb + 1) * TB, :] = jnp.broadcast_to(
                to_column(vec[rb : rb + 1, :]), (TB, TB)
            )

    slot = lax.broadcasted_iota(jnp.int32, (TB, TB), 1)
    which = lax.broadcasted_iota(jnp.int32, (TB, TB), 0)
    live = slot < count_ref[0, 0]
    row_hot = jnp.where((rows_ref[...] == which) & live, 1.0, 0.0).astype(BF16)
    col_hot = jnp.where((cols_ref[...] == which) & live, 1.0, 0.0).astype(BF16)
    present = nt_dot(row_hot[:NB], col_hot).astype(BF16)
    for cb in range(NB):
        spread = jnp.where(which == cb, 1.0, 0.0).astype(BF16)
        hits = jnp.dot(present, spread, preferred_element_type=F32)
        bias[:, cb * TB : (cb + 1) * TB] = jnp.where(hits > 0.5, 0.0, MASKED)

    @pl.loop(0, NB // 2)
    def _(rb):
        top = None
        left = src[block(rb, 2 * TB), :]
        for cb in range(NB // 2):
            at = slice(cb * 2 * TB, (cb + 1) * 2 * TB)
            s = nt_dot(left, tgt[at, :])
            for half in range(2):
                line = bias[pl.ds(rb * 2 + half, 1), at]
                q[block(rb * 2 + half), at] = s[half * TB : (half + 1) * TB] + line
        for half in range(2):
            here = block(rb * 2 + half)
            top = q[here, 0:TB]
            for cb in range(1, NB):
                top = jnp.maximum(top, q[here, cb * TB : (cb + 1) * TB])
            total = jnp.exp(q[here, 0:TB] - top)
            for cb in range(1, NB):
                total += jnp.exp(q[here, cb * TB : (cb + 1) * TB] - top)
            wide[here, :] = top
            wide2[here, :] = total

    for rb in range(NB):
        here = slice(rb * TB, (rb + 1) * TB)
        top = wide[here, :]
        largest = jnp.max(top, axis=1, keepdims=True)
        total = jnp.sum(wide2[here, :] * jnp.exp(top - largest), axis=1, keepdims=True)
        part[0, rb : rb + 1, :] = to_row(largest + jnp.log(total))

    pl.semaphore_wait(barrier, 2 * (NB - 1))

    def start_reduce(index, axis):
        me = row_me if axis == "row" else col_me

        @pl.loop(0, NB - 1)
        def _(k):
            if axis == "row":
                j = k // 2
                far = lax.rem(4 + (1 - 2 * (j % 2)) * ((j + 1) // 2), 8)
                peer = lax.rem(z_me + far, 8) * 2 + lax.rem(core + 1 + k, 2)
            else:
                j = k // 4
                dy = lax.rem(2 + (1 - 2 * (j % 2)) * ((j + 1) // 2), 4)
                i = k % 4
                dx = lax.rem(2 + (1 - 2 * (i % 2)) * ((i + 1) // 2), 4)
                peer = lax.rem(y_me + dy, 4) * 4 + lax.rem(x_me + dx, 4)
            pltpu.make_async_remote_copy(
                src_ref=part.at[index],
                dst_ref=land.at[index, me],
                send_sem=ar_send.at[index],
                recv_sem=ar_recv.at[index],
                device_id={axis: peer},
                device_id_type=MESH,
            ).start()

        land[index, me] = part[index]

    def end_reduce(index):
        others = land.at[index, pl.ds(0, NB - 1)]
        pltpu.make_async_copy(others, others, ar_recv.at[index]).wait()

    def summed(index):
        end_reduce(index)
        terms = [land[index, k] for k in range(NB)]
        while len(terms) > 1:
            terms = [terms[k] + terms[k + 1] for k in range(0, len(terms), 2)]
        return terms[0]

    def log_summed(index):
        end_reduce(index)
        largest = land[index, 0]
        for k in range(1, NB):
            largest = jnp.maximum(largest, land[index, k])
        total = jnp.exp(land[index, 0] - largest)
        for k in range(1, NB):
            total += jnp.exp(land[index, k] - largest)
        return largest + jnp.log(total)

    def row_pass(weights, index):
        vec_w[...] = weights

        @pl.loop(0, NB)
        def _(rb):
            here = block(rb)
            total = q[here, 0:TB] * vec_w[0:1, :]
            for cb in range(1, NB):
                total += q[here, cb * TB : (cb + 1) * TB] * vec_w[cb : cb + 1, :]
            wide[here, :] = total

        for rb in range(NB):
            total = jnp.sum(wide[rb * TB : (rb + 1) * TB, :], axis=1, keepdims=True)
            part[index, rb : rb + 1, :] = to_row(total)
        start_reduce(index, "col")

    def fold(value):
        total = value[0:8]
        for k in range(1, NB):
            total += value[k * 8 : (k + 1) * 8]
        return total

    def col_pass(weights, scale, index):
        widen(weights)

        def body(rb, totals):
            here = block(rb)
            u = wide[here, :]
            return tuple(
                totals[cb] + fold(q[here, cb * TB : (cb + 1) * TB] * u) for cb in range(NB)
            )

        totals = lax.fori_loop(0, NB, body, (jnp.zeros((8, TB), F32),) * NB)
        for cb in range(NB):
            vec[cb : cb + 1, :] = jnp.sum(totals[cb], axis=0, keepdims=True)
        part[index] = vec[...] * scale
        start_reduce(index, "row")

    start_reduce(0, "col")
    unit = jnp.where(
        lax.broadcasted_iota(jnp.int32, (E, E), 0) == lax.broadcasted_iota(jnp.int32, (E, E), 1),
        1.0,
        0.0,
    ).astype(BF16)
    for cb in range(NB // 2):
        at = slice(cb * 2 * TB, (cb + 1) * 2 * TB)
        srct[:, at] = nt_dot(unit, src[at, :]).astype(BF16)
    a = a_ref[...]
    b = b_ref[...]
    f1 = a - log_summed(0)

    widen(f1)

    def top_body(rb, tops):
        here = block(rb)
        u = wide[here, :]
        out = []
        for cb in range(NB):
            moved = q[here, cb * TB : (cb + 1) * TB] + u
            top = tops[cb]
            for k in range(NB):
                top = jnp.maximum(top, moved[k * 8 : (k + 1) * 8])
            out.append(top)
        return tuple(out)

    tops = lax.fori_loop(0, NB, top_body, (jnp.full((8, TB), MASKED, F32),) * NB)
    for cb in range(NB):
        vec_w[cb : cb + 1, :] = jnp.max(tops[cb], axis=0, keepdims=True)
    c = vec_w[...]

    def exp_body(rb, totals):
        here = block(rb)
        u = wide[here, :]
        out = []
        for cb in range(NB):
            at = slice(cb * TB, (cb + 1) * TB)
            value = jnp.exp((q[here, at] + u) - vec_w[cb : cb + 1, :])
            q[here, at] = value
            out.append(totals[cb] + fold(value))
        return tuple(out)

    totals = lax.fori_loop(0, NB, exp_body, (jnp.zeros((8, TB), F32),) * NB)
    for cb in range(NB):
        vec[cb : cb + 1, :] = jnp.sum(totals[cb], axis=0, keepdims=True)
    part[1] = c + jnp.log(vec[...])
    start_reduce(1, "row")
    exp_a = jnp.exp(a)
    exp_b = jnp.exp(b)
    inv_a = jnp.exp(-a)
    inv_b = jnp.exp(-b)
    g1 = b - log_summed(1)

    d = jnp.exp(c + g1)

    def put(ref, term, value):
        vec[...] = value
        for k in range(NB):
            ref[k * 8 + term : k * 8 + term + 1, :] = vec[k : k + 1, :]

    xs[...] = jnp.zeros_like(xs)
    ys[...] = jnp.zeros_like(ys)

    row_pass(d, 2)
    put(ys, 4, d * -SHRINK)
    put(ys, 5, jnp.exp(c) * -SHRINK)
    put(xs, 2, jnp.ones_like(a))
    u2 = exp_a / summed(2)
    col_pass(u2, d, 3)
    put(xs, 1, u2)
    v2 = exp_b / summed(3)
    dv2 = d * v2
    row_pass(dv2, 4)
    put(ys, 3, dv2 * -SHRINK)
    u3 = exp_a / summed(4)
    col_pass(u3, d, 5)
    put(xs, 0, u3)
    f_out[...] = f1 + jnp.log(u3)
    v3 = exp_b / summed(5)

    y3 = d * v3 * inv_b * cc_ref[...]
    row_pass(y3, 6)
    put(ys, 0, y3 * -SHRINK)
    g_out[...] = g1 + jnp.log(v3)
    x3 = u3 * inv_a * (rc_ref[...] - u3 * summed(6))
    col_pass(x3, d, 7)
    put(xs, 3, x3)
    y2 = dv2 * inv_b * (-v2 * summed(7))
    row_pass(y2, 8)
    put(ys, 1, y2 * -SHRINK)
    x2 = u2 * inv_a * (-u2 * summed(8))
    col_pass(x2, d, 9)
    put(xs, 4, x2)
    y1 = d * inv_b * -summed(9)
    row_pass(y1, 10)
    put(ys, 2, y1 * -SHRINK)

    def thirds(value):
        first = value.astype(BF16).astype(F32)
        rest = value - first
        second = rest.astype(BF16).astype(F32)
        third = (rest - second).astype(BF16).astype(F32)
        return first, second, third

    def stacked(ref, to, order):
        for k in range(NB):
            parts = thirds(ref[k * 8 : (k + 1) * 8, :])
            to[:, k * TB : (k + 1) * TB] = jnp.concatenate(
                [parts[i] for i in order], axis=0
            ).astype(BF16)

    stacked(ys, yb, (0, 1, 0, 2, 0, 1))
    put(xs, 5, inv_a * -summed(10))
    stacked(xs, xb, (0, 0, 1, 0, 2, 1))

    @pl.loop(0, NB // 2)
    def _(k):
        j = lax.rem(col_me // 2 + 1 + k, NB // 2)
        here = block(j, 2 * TB)
        left = nt_dot(unit, xb[:, here]).astype(BF16)
        for cb in range(NB // 2):
            at = slice(cb * 2 * TB, (cb + 1) * 2 * TB)
            factor = jnp.dot(left, yb[:, at], preferred_element_type=F32)
            w[here, at] = (q[here, at] * factor).astype(BF16)
        total = jnp.dot(w[here, :], tgt[...], preferred_element_type=F32)
        for half in range(2):
            peer = j * 2 + half
            gs_send[peer] = total[half * TB : (half + 1) * TB]

            @pl.when(peer != col_me)
            def _():
                pltpu.make_async_remote_copy(
                    src_ref=gs_send.at[peer],
                    dst_ref=gs_land.at[col_me],
                    send_sem=gs_ssem,
                    recv_sem=gs_rsem,
                    device_id={"col": peer},
                    device_id_type=MESH,
                ).start()

    gs_land[col_me] = gs_send[col_me]

    def chip_at(k):
        return lax.rem(z_me + 4 + (1 - 2 * (k % 2)) * ((k + 1) // 2), 8)

    def sibling_copy(j):
        return pltpu.make_async_remote_copy(
            src_ref=gt_part.at[j, 1 - core],
            dst_ref=gt_sib.at[j],
            send_sem=sib_ssem.at[j],
            recv_sem=sib_rsem.at[j],
            device_id={"row": z_me * 2 + 1 - core},
            device_id_type=MESH,
        )

    def pass_on(k):
        j = chip_at(k)
        sibling_copy(j).wait_recv()
        gt_send[j] = gt_part[j, core] + gt_sib[j]

        @pl.when(j != z_me)
        def _():
            pltpu.make_async_remote_copy(
                src_ref=gt_send.at[j],
                dst_ref=gt_land.at[z_me],
                send_sem=gt_ssem,
                recv_sem=gt_rsem,
                device_id={"row": j * 2 + core},
                device_id_type=MESH,
            ).start()

    @pl.loop(0, 8)
    def _(k):
        j = chip_at(k)
        total = jnp.dot(srct[...], w[:, block(j, 2 * TB)], preferred_element_type=F32)
        gt_part[j, 0] = total[:, :TB]
        gt_part[j, 1] = total[:, TB:]
        sibling_copy(j).start()

        @pl.when(k > 0)
        def _():
            pass_on(k - 1)

    pass_on(7)
    gt_land[z_me] = gt_send[z_me]

    others = gs_land.at[pl.ds(0, NB - 1)]
    pltpu.make_async_copy(others, others, gs_rsem).wait()
    for k in range(NB):
        at = slice(k * 8, (k + 1) * 8)
        total = gs_land[0, at, :]
        for i in range(1, NB):
            total += gs_land[i, at, :]
        gs_out[at, :] = total * GROW

    others = gt_land.at[pl.ds(0, 7)]
    pltpu.make_async_copy(others, others, gt_rsem).wait()
    for k in range(NB):
        at = slice(k * 16, (k + 1) * 16)
        total = gt_land[0, at, :]
        for i in range(1, 8):
            total += gt_land[i, at, :]
        gt_out[at, :] = total * GROW

    @pl.loop(0, ROUNDS)
    def _(index):
        others = land.at[index, pl.ds(0, NB - 1)]
        pltpu.make_async_copy(others, others, ar_send.at[index]).wait()

    @pl.loop(0, 8)
    def _(j):
        sibling_copy(j).wait_send()

    others = gs_land.at[pl.ds(0, NB - 1)]
    pltpu.make_async_copy(others, others, gs_ssem).wait()
    others = gt_land.at[pl.ds(0, 7)]
    pltpu.make_async_copy(others, others, gt_ssem).wait()


def on_device(src, tgt, a, b, rows, cols, counts, rc, cc):
    vmem = pl.BlockSpec(memory_space=pltpu.VMEM)
    smem = pl.BlockSpec(memory_space=pltpu.SMEM)
    dma = pltpu.SemaphoreType.DMA
    f, g, gs, gt = pl.pallas_call(
        kernel,
        out_shape=(
            jax.ShapeDtypeStruct((NB, TB), F32),
            jax.ShapeDtypeStruct((NB, TB), F32),
            jax.ShapeDtypeStruct((TB, E), F32),
            jax.ShapeDtypeStruct((E, TB), F32),
        ),
        in_specs=[vmem] * 6 + [smem] + [vmem] * 2,
        out_specs=(vmem,) * 4,
        scratch_shapes=[
            pltpu.VMEM((CELLS, CELLS), F32),
            pltpu.VMEM((CELLS, CELLS), BF16),
            pltpu.VMEM((ROUNDS, NB, TB), F32),
            pltpu.VMEM((ROUNDS, NB, NB, TB), F32),
            pltpu.VMEM((CELLS, TB), F32),
            pltpu.VMEM((CELLS, TB), F32),
            pltpu.VMEM((NB, CELLS), F32),
            pltpu.VMEM((NB, TB), F32),
            pltpu.VMEM((NB, TB), F32),
            pltpu.VMEM((E, CELLS), BF16),
            pltpu.VMEM((NB * 8, TB), F32),
            pltpu.VMEM((NB * 8, TB), F32),
            pltpu.VMEM((48, CELLS), BF16),
            pltpu.VMEM((48, CELLS), BF16),
            pltpu.VMEM((NB, TB, E), F32),
            pltpu.VMEM((NB, TB, E), F32),
            pltpu.VMEM((8, 2, E, TB), F32),
            pltpu.VMEM((8, E, TB), F32),
            pltpu.VMEM((8, E, TB), F32),
            pltpu.VMEM((8, E, TB), F32),
            dma((ROUNDS,)),
            dma((ROUNDS,)),
            dma,
            dma,
            dma((8,)),
            dma((8,)),
            dma,
            dma,
        ],
        compiler_params=pltpu.CompilerParams(
            collective_id=0, has_side_effects=True, vmem_limit_bytes=56 << 20
        ),
    )(
        src,
        tgt,
        a.reshape(NB, TB),
        b.reshape(NB, TB),
        rows.reshape(1, TB),
        cols.reshape(1, TB),
        counts,
        rc.reshape(NB, TB),
        cc.reshape(NB, TB),
    )
    return f.reshape(CELLS), g.reshape(CELLS), gs, gt.T


def solution(mesh):
    placed = (
        P("row", None),
        P("col", None),
        P("row"),
        P("col"),
        P("row", "col", None),
        P("row", "col", None),
        P("row", "col"),
        P("row"),
        P("col"),
    )
    return jax.shard_map(
        on_device,
        mesh=mesh,
        in_specs=placed,
        out_specs=(P("row"), P("col"), P(("row", "col"), None), P(("col", "row"), None)),
        check_vma=False,
    )
```

```python
import jax
import jax.numpy as jnp
from jax import lax
from jax.experimental import pallas as pl
from jax.experimental.pallas import tpu as pltpu
from jax.sharding import PartitionSpec as P

MESH = pl.DeviceIdType.MESH
TB = 128
NB = 16
CELLS = NB * TB
E = 256
ROUNDS = 11
HALF = TB // 2
SUBS = 4
SUB = E // SUBS
MASKED = -1e30
F32 = jnp.float32
BF16 = jnp.bfloat16
SHRINK = 2.0**-40
GROW = 2.0**40


def nt_dot(x, y):
    return lax.dot_general(x, y, (((1,), (1,)), ((), ())), preferred_element_type=F32)


def tn_dot(x, y):
    return lax.dot_general(x, y, (((0,), (0,)), ((), ())), preferred_element_type=F32)


def block(index, size=TB):
    return pl.ds(pl.multiple_of(index * size, size), size)


def kernel(
    src, tgt, a_ref, b_ref, rows_ref, cols_ref, count_ref, rc_ref, cc_ref,
    f_out, g_out, gs_out, gt_out,
    q, w, w_cols, part, land, wide, wide2, bias, vec, vec_w, srct, xs, ys, xb, yb, xt,
    gs_sum, gs_last, gs_land, gs_mid, gs_land2, gt_part, gt_sib, gt_sum, gt_land,
    ar_send, ar_recv, gs_ssem, gs_rsem, gs_ssem2, gs_rsem2, sib_ssem, sib_rsem, gt_ssem, gt_rsem,
):
    row_me = lax.axis_index("row")
    col_me = lax.axis_index("col")
    z_me = row_me // 2
    core = row_me % 2
    y_me = col_me // 4
    x_me = col_me % 4

    barrier = pltpu.get_barrier_semaphore()

    @pl.loop(1, NB)
    def _(k):
        pl.semaphore_signal(
            barrier, inc=1, device_id={"row": lax.rem(row_me + k, NB)}, device_id_type=MESH
        )
        pl.semaphore_signal(
            barrier, inc=1, device_id={"col": lax.rem(col_me + k, NB)}, device_id_type=MESH
        )

    eye = lax.broadcasted_iota(jnp.int32, (TB, TB), 0) == lax.broadcasted_iota(
        jnp.int32, (TB, TB), 1
    )

    def to_row(column):
        return jnp.sum(jnp.where(eye, column, 0.0), axis=0, keepdims=True)

    def to_column(row):
        return jnp.sum(jnp.where(eye, row, 0.0), axis=1, keepdims=True)

    def widen(value):
        vec[...] = value
        for rb in range(NB):
            wide[rb * TB : (rb + 1) * TB, :] = jnp.broadcast_to(
                to_column(vec[rb : rb + 1, :]), (TB, TB)
            )

    slot = lax.broadcasted_iota(jnp.int32, (TB, TB), 1)
    which = lax.broadcasted_iota(jnp.int32, (TB, TB), 0)
    live = slot < count_ref[0, 0]
    row_hot = jnp.where((rows_ref[...] == which) & live, 1.0, 0.0).astype(BF16)
    col_hot = jnp.where((cols_ref[...] == which) & live, 1.0, 0.0).astype(BF16)
    present = nt_dot(row_hot[:NB], col_hot).astype(BF16)
    for cb in range(NB):
        spread = jnp.where(which == cb, 1.0, 0.0).astype(BF16)
        hits = jnp.dot(present, spread, preferred_element_type=F32)
        bias[:, cb * TB : (cb + 1) * TB] = jnp.where(hits > 0.5, 0.0, MASKED)

    @pl.loop(0, NB // 2)
    def _(rb):
        top = None
        left = src[block(rb, 2 * TB), :]
        for cb in range(NB // 2):
            at = slice(cb * 2 * TB, (cb + 1) * 2 * TB)
            s = nt_dot(left, tgt[at, :])
            for half in range(2):
                line = bias[pl.ds(rb * 2 + half, 1), at]
                q[block(rb * 2 + half), at] = s[half * TB : (half + 1) * TB] + line
        for half in range(2):
            here = block(rb * 2 + half)
            top = q[here, 0:TB]
            for cb in range(1, NB):
                top = jnp.maximum(top, q[here, cb * TB : (cb + 1) * TB])
            total = jnp.exp(q[here, 0:TB] - top)
            for cb in range(1, NB):
                total += jnp.exp(q[here, cb * TB : (cb + 1) * TB] - top)
            wide[here, :] = top
            wide2[here, :] = total

    for rb in range(NB):
        here = slice(rb * TB, (rb + 1) * TB)
        top = wide[here, :]
        largest = jnp.max(top, axis=1, keepdims=True)
        total = jnp.sum(wide2[here, :] * jnp.exp(top - largest), axis=1, keepdims=True)
        part[0, rb : rb + 1, :] = to_row(largest + jnp.log(total))

    pl.semaphore_wait(barrier, 2 * (NB - 1))

    def start_reduce(index, axis):
        me = row_me if axis == "row" else col_me

        @pl.loop(0, NB - 1)
        def _(k):
            if axis == "row":
                j = k // 2
                far = lax.rem(4 + (1 - 2 * (j % 2)) * ((j + 1) // 2), 8)
                peer = lax.rem(z_me + far, 8) * 2 + lax.rem(core + 1 + k, 2)
            else:
                j = k // 4
                dy = lax.rem(2 + (1 - 2 * (j % 2)) * ((j + 1) // 2), 4)
                i = k % 4
                dx = lax.rem(2 + (1 - 2 * (i % 2)) * ((i + 1) // 2), 4)
                peer = lax.rem(y_me + dy, 4) * 4 + lax.rem(x_me + dx, 4)
            pltpu.make_async_remote_copy(
                src_ref=part.at[index],
                dst_ref=land.at[index, me],
                send_sem=ar_send.at[index],
                recv_sem=ar_recv.at[index],
                device_id={axis: peer},
                device_id_type=MESH,
            ).start()

        land[index, me] = part[index]

    def end_reduce(index):
        others = land.at[index, pl.ds(0, NB - 1)]
        pltpu.make_async_copy(others, others, ar_recv.at[index]).wait()

    def summed(index):
        end_reduce(index)
        terms = [land[index, k] for k in range(NB)]
        while len(terms) > 1:
            terms = [terms[k] + terms[k + 1] for k in range(0, len(terms), 2)]
        return terms[0]

    def log_summed(index):
        end_reduce(index)
        largest = land[index, 0]
        for k in range(1, NB):
            largest = jnp.maximum(largest, land[index, k])
        total = jnp.exp(land[index, 0] - largest)
        for k in range(1, NB):
            total += jnp.exp(land[index, k] - largest)
        return largest + jnp.log(total)

    def row_pass(weights, index):
        vec_w[...] = weights

        @pl.loop(0, NB)
        def _(rb):
            here = block(rb)
            total = q[here, 0:TB] * vec_w[0:1, :]
            for cb in range(1, NB):
                total += q[here, cb * TB : (cb + 1) * TB] * vec_w[cb : cb + 1, :]
            wide[here, :] = total

        for rb in range(NB):
            total = jnp.sum(wide[rb * TB : (rb + 1) * TB, :], axis=1, keepdims=True)
            part[index, rb : rb + 1, :] = to_row(total)
        start_reduce(index, "col")

    def fold(value):
        total = value[0:8]
        for k in range(1, NB):
            total += value[k * 8 : (k + 1) * 8]
        return total

    def col_pass(weights, scale, index):
        widen(weights)

        def body(rb, totals):
            here = block(rb)
            u = wide[here, :]
            return tuple(
                totals[cb] + fold(q[here, cb * TB : (cb + 1) * TB] * u) for cb in range(NB)
            )

        totals = lax.fori_loop(0, NB, body, (jnp.zeros((8, TB), F32),) * NB)
        for cb in range(NB):
            vec[cb : cb + 1, :] = jnp.sum(totals[cb], axis=0, keepdims=True)
        part[index] = vec[...] * scale
        start_reduce(index, "row")

    start_reduce(0, "col")
    unit = jnp.where(
        lax.broadcasted_iota(jnp.int32, (E, E), 0) == lax.broadcasted_iota(jnp.int32, (E, E), 1),
        1.0,
        0.0,
    ).astype(BF16)
    for cb in range(NB // 2):
        at = slice(cb * 2 * TB, (cb + 1) * 2 * TB)
        srct[:, at] = nt_dot(unit, src[at, :]).astype(BF16)
    a = a_ref[...]
    b = b_ref[...]
    f1 = a - log_summed(0)

    widen(f1)

    def top_body(rb, tops):
        here = block(rb)
        u = wide[here, :]
        out = []
        for cb in range(NB):
            moved = q[here, cb * TB : (cb + 1) * TB] + u
            top = tops[cb]
            for k in range(NB):
                top = jnp.maximum(top, moved[k * 8 : (k + 1) * 8])
            out.append(top)
        return tuple(out)

    tops = lax.fori_loop(0, NB, top_body, (jnp.full((8, TB), MASKED, F32),) * NB)
    for cb in range(NB):
        vec_w[cb : cb + 1, :] = jnp.max(tops[cb], axis=0, keepdims=True)
    c = vec_w[...]

    def exp_body(rb, totals):
        here = block(rb)
        u = wide[here, :]
        out = []
        for cb in range(NB):
            at = slice(cb * TB, (cb + 1) * TB)
            value = jnp.exp((q[here, at] + u) - vec_w[cb : cb + 1, :])
            q[here, at] = value
            out.append(totals[cb] + fold(value))
        return tuple(out)

    totals = lax.fori_loop(0, NB, exp_body, (jnp.zeros((8, TB), F32),) * NB)
    for cb in range(NB):
        vec[cb : cb + 1, :] = jnp.sum(totals[cb], axis=0, keepdims=True)
    part[1] = c + jnp.log(vec[...])
    start_reduce(1, "row")
    exp_a = jnp.exp(a)
    exp_b = jnp.exp(b)
    inv_a = jnp.exp(-a)
    inv_b = jnp.exp(-b)
    g1 = b - log_summed(1)

    d = jnp.exp(c + g1)

    def put(ref, term, value):
        vec[...] = value
        for k in range(NB):
            ref[k * 8 + term : k * 8 + term + 1, :] = vec[k : k + 1, :]

    xs[...] = jnp.zeros_like(xs)
    ys[...] = jnp.zeros_like(ys)

    def thirds(value):
        first = value.astype(BF16).astype(F32)
        rest = value - first
        second = rest.astype(BF16).astype(F32)
        third = (rest - second).astype(BF16).astype(F32)
        return first, second, third

    def stacked(ref, to, order):
        for k in range(NB):
            parts = thirds(ref[k * 8 : (k + 1) * 8, :])
            to[:, k * TB : (k + 1) * TB] = jnp.concatenate(
                [parts[i] for i in order], axis=0
            ).astype(BF16)

    def stack_x():
        stacked(xs, xb, (0, 0, 1, 0, 2, 1))
        for k in range(NB // 2):
            at = slice(k * 2 * TB, (k + 1) * 2 * TB)
            xt[at, :] = nt_dot(unit, xb[:, at]).astype(BF16)

    def stack_y():
        stacked(ys, yb, (0, 1, 0, 2, 0, 1))

    def source_product(into, line, add):
        if line is not None:
            vec_w[...] = line

        @pl.loop(0, NB // 4)
        def _(k):
            here = block(k, 4 * TB)
            for cb in range(NB // 2):
                at = slice(cb * 2 * TB, (cb + 1) * 2 * TB)
                if line is None:
                    factor = jnp.dot(xt[here, :], yb[:, at], preferred_element_type=F32)
                    w[:, at] = (q[here, at] * factor).astype(BF16)
                else:
                    for half in range(2):
                        col = slice((cb * 2 + half) * TB, (cb * 2 + half + 1) * TB)
                        factor = vec_w[cb * 2 + half : cb * 2 + half + 1, :]
                        w[:, col] = (q[here, col] * factor).astype(BF16)
            total = jnp.dot(w[...], tgt[...], preferred_element_type=F32)
            if add:
                into[here, :] += total
            else:
                into[here, :] = total

    row_pass(d, 2)
    put(ys, 4, d * -SHRINK)
    put(ys, 5, jnp.exp(c) * -SHRINK)
    put(xs, 2, jnp.ones_like(a))
    u2 = exp_a / summed(2)
    col_pass(u2, d, 3)
    put(xs, 1, u2)
    source_product(gs_last, jnp.exp(c) * -SHRINK, False)
    v2 = exp_b / summed(3)
    dv2 = d * v2
    row_pass(dv2, 4)
    put(ys, 3, dv2 * -SHRINK)
    u3 = exp_a / summed(4)
    col_pass(u3, d, 5)
    put(xs, 0, u3)
    f_out[...] = f1 + jnp.log(u3)
    v3 = exp_b / summed(5)

    y3 = d * v3 * inv_b * cc_ref[...]
    row_pass(y3, 6)
    put(ys, 0, y3 * -SHRINK)
    g_out[...] = g1 + jnp.log(v3)
    x3 = u3 * inv_a * (rc_ref[...] - u3 * summed(6))
    col_pass(x3, d, 7)
    put(xs, 3, x3)
    y2 = dv2 * inv_b * (-v2 * summed(7))
    row_pass(y2, 8)
    put(ys, 1, y2 * -SHRINK)
    x2 = u2 * inv_a * (-u2 * summed(8))
    col_pass(x2, d, 9)
    put(xs, 4, x2)
    stack_x()
    stack_y()
    source_product(gs_sum, None, False)
    y1 = d * inv_b * -summed(9)
    row_pass(y1, 10)
    put(ys, 2, y1 * -SHRINK)
    stack_y()
    source_product(gs_sum, y1 * -SHRINK, True)
    x1 = inv_a * -summed(10)
    put(xs, 5, x1)

    widen(x1)

    def first_copy(half, other, k):
        if half == 0:
            to_x = lax.rem(x_me + k, 4)
            owner, peer = other * 4 + to_x, y_me * 4 + to_x
        else:
            to_y = lax.rem(y_me + k, 4)
            owner, peer = to_y * 4 + other, to_y * 4 + x_me
        rows = pl.ds(pl.multiple_of(owner * TB + half * HALF, HALF), HALF)
        return pltpu.make_async_remote_copy(
            src_ref=gs_sum.at[rows],
            dst_ref=gs_land.at[half, other, x_me if half == 0 else y_me],
            send_sem=gs_ssem.at[half],
            recv_sem=gs_rsem.at[half, other],
            device_id={"col": peer},
            device_id_type=MESH,
        )

    @pl.loop(0, NB)
    def _(rb):
        here = block(rb)
        u = wide[here, :]
        for half in range(2):
            at = slice(half * TB, (half + 1) * TB)
            gs_sum[here, at] += u * gs_last[here, at]

    def other_at(half, k):
        return lax.rem((y_me if half == 0 else x_me) + 2 + (1 - 2 * (k % 2)) * ((k + 1) // 2), 4)

    @pl.loop(0, 4)
    def _(k):
        for half in range(2):
            for far in (2, 1, 3):
                first_copy(half, other_at(half, k), far).start()

    def second_stage(k):
        for half in range(2):
            other = other_at(half, k)
            others = gs_land.at[half, other, pl.ds(0, 3)]
            pltpu.make_async_copy(others, others, gs_rsem.at[half, other]).wait()
            mine = x_me if half == 0 else y_me
            owner = other * 4 + x_me if half == 0 else y_me * 4 + other
            rows = pl.ds(pl.multiple_of(owner * TB + half * HALF, HALF), HALF)
            total = gs_sum[rows, :]
            for far in range(1, 4):
                total += gs_land[half, other, lax.rem(mine + far, 4)]
            gs_mid[half, other] = total

            @pl.when(k < 3)
            def _():
                peer = other * 4 + x_me if half == 0 else y_me * 4 + other
                pltpu.make_async_remote_copy(
                    src_ref=gs_mid.at[half, other],
                    dst_ref=gs_land2.at[half, y_me if half == 0 else x_me],
                    send_sem=gs_ssem2.at[half],
                    recv_sem=gs_rsem2.at[half],
                    device_id={"col": peer},
                    device_id_type=MESH,
                ).start()

    stack_x()

    def chip_at(k):
        return lax.rem(z_me + 4 + (1 - 2 * (k % 2)) * ((k + 1) // 2), 8)

    def sibling_copy(j):
        return pltpu.make_async_remote_copy(
            src_ref=gt_part.at[j, 1 - core],
            dst_ref=gt_sib.at[j],
            send_sem=sib_ssem.at[j],
            recv_sem=sib_rsem.at[j],
            device_id={"row": z_me * 2 + 1 - core},
            device_id_type=MESH,
        )

    def ring_copy(way, step, sub):
        j = lax.rem(z_me + jnp.where(way == 0, 4 - step, 4 + step), 8)
        rows = pl.ds(sub * SUB, SUB)
        peer = lax.rem(z_me + jnp.where(way == 0, 1, 7), 8)
        return pltpu.make_async_remote_copy(
            src_ref=gt_sum.at[j, rows],
            dst_ref=gt_land.at[way, step, rows],
            send_sem=gt_ssem.at[way, step, sub],
            recv_sem=gt_rsem.at[way, step, sub],
            device_id={"row": peer * 2 + core},
            device_id_type=MESH,
        )

    def ready(k):
        j = chip_at(k)
        sibling_copy(j).wait_recv()
        gt_sum[j] = gt_part[j, core] + gt_sib[j]

    def advance(k):
        ready(k)
        j = chip_at(k)
        way = (k + 1) % 2
        step = (k + 1) // 2
        for sub in range(SUBS):
            rows = pl.ds(sub * SUB, SUB)

            @pl.when((step > 1) | (way == sub // (SUBS // 2)))
            def _():
                ring_copy(way, step - 1, sub).wait_recv()
                gt_sum[j, rows] += gt_land[way, step - 1, rows]

            ring_copy(way, step, sub).start()

    @pl.loop(0, 8)
    def _(k):
        j = chip_at(k)
        cols = block(j, 2 * TB)
        for part_k in range(NB // 4):
            here = slice(part_k * 4 * TB, (part_k + 1) * 4 * TB)
            factor = jnp.dot(xt[here, :], yb[:, cols], preferred_element_type=F32)
            w_cols[here, :] = (q[here, cols] * factor).astype(BF16)
        total = jnp.dot(srct[...], w_cols[...], preferred_element_type=F32)
        gt_part[j, 0] = total[:, :TB]
        gt_part[j, 1] = total[:, TB:]
        sibling_copy(j).start()

        @pl.when(k == 1)
        def _():
            ready(0)
            for sub in range(SUBS):
                ring_copy(sub // (SUBS // 2), 0, sub).start()

        @pl.when(k > 1)
        def _():
            advance(k - 1)

        @pl.when(k > 4)
        def _():
            second_stage(k - 5)

    ready(7)
    second_stage(3)

    for way in range(2):
        for sub in range(SUBS):
            ring_copy(way, 3, sub).wait_recv()
    for k in range(2):
        at = slice(k * TB, (k + 1) * TB)
        total = gt_sum[z_me, at, :] + gt_land[0, 3, at, :] + gt_land[1, 3, at, :]
        gt_out[:, at] = (total * GROW).T

    for half in range(2):
        others = gs_land2.at[half, pl.ds(0, 3)]
        pltpu.make_async_copy(others, others, gs_rsem2.at[half]).wait()
        mine = y_me if half == 0 else x_me
        total = gs_mid[half, mine]
        for far in range(1, 4):
            total += gs_land2[half, lax.rem(mine + far, 4)]
        gs_out[half * HALF : (half + 1) * HALF, :] = total * GROW

    @pl.loop(0, ROUNDS)
    def _(index):
        others = land.at[index, pl.ds(0, NB - 1)]
        pltpu.make_async_copy(others, others, ar_send.at[index]).wait()

    for half in range(2):
        others = gs_land.at[half, pl.ds(0, 3)]
        pltpu.make_async_copy(others, others, gs_ssem.at[half]).wait()
        others = gs_land2.at[half, pl.ds(0, 3)]
        pltpu.make_async_copy(others, others, gs_ssem2.at[half]).wait()

    @pl.loop(0, 8)
    def _(j):
        sibling_copy(j).wait_send()

    for sub in range(SUBS):
        ring_copy(sub // (SUBS // 2), 0, sub).wait_send()
        for way in range(2):
            for step in range(1, 4):
                ring_copy(way, step, sub).wait_send()


def on_device(src, tgt, a, b, rows, cols, counts, rc, cc):
    vmem = pl.BlockSpec(memory_space=pltpu.VMEM)
    smem = pl.BlockSpec(memory_space=pltpu.SMEM)
    dma = pltpu.SemaphoreType.DMA
    f, g, gs, gt = pl.pallas_call(
        kernel,
        out_shape=(
            jax.ShapeDtypeStruct((NB, TB), F32),
            jax.ShapeDtypeStruct((NB, TB), F32),
            jax.ShapeDtypeStruct((TB, E), F32),
            jax.ShapeDtypeStruct((TB, E), F32),
        ),
        in_specs=[vmem] * 6 + [smem] + [vmem] * 2,
        out_specs=(vmem,) * 4,
        scratch_shapes=[
            pltpu.VMEM((CELLS, CELLS), F32),
            pltpu.VMEM((4 * TB, CELLS), BF16),
            pltpu.VMEM((CELLS, 2 * TB), BF16),
            pltpu.VMEM((ROUNDS, NB, TB), F32),
            pltpu.VMEM((ROUNDS, NB, NB, TB), F32),
            pltpu.VMEM((CELLS, TB), F32),
            pltpu.VMEM((CELLS, TB), F32),
            pltpu.VMEM((NB, CELLS), F32),
            pltpu.VMEM((NB, TB), F32),
            pltpu.VMEM((NB, TB), F32),
            pltpu.VMEM((E, CELLS), BF16),
            pltpu.VMEM((NB * 8, TB), F32),
            pltpu.VMEM((NB * 8, TB), F32),
            pltpu.VMEM((48, CELLS), BF16),
            pltpu.VMEM((48, CELLS), BF16),
            pltpu.VMEM((CELLS, 48), BF16),
            pltpu.VMEM((CELLS, E), F32),
            pltpu.VMEM((CELLS, E), F32),
            pltpu.VMEM((2, 4, 4, HALF, E), F32),
            pltpu.VMEM((2, 4, HALF, E), F32),
            pltpu.VMEM((2, 4, HALF, E), F32),
            pltpu.VMEM((8, 2, E, TB), F32),
            pltpu.VMEM((8, E, TB), F32),
            pltpu.VMEM((8, E, TB), F32),
            pltpu.VMEM((2, 4, E, TB), F32),
            dma((ROUNDS,)),
            dma((ROUNDS,)),
            dma((2,)),
            dma((2, 4)),
            dma((2,)),
            dma((2,)),
            dma((8,)),
            dma((8,)),
            dma((2, 4, SUBS)),
            dma((2, 4, SUBS)),
        ],
        compiler_params=pltpu.CompilerParams(
            collective_id=0, has_side_effects=True, vmem_limit_bytes=56 << 20
        ),
    )(
        src,
        tgt,
        a.reshape(NB, TB),
        b.reshape(NB, TB),
        rows.reshape(1, TB),
        cols.reshape(1, TB),
        counts,
        rc.reshape(NB, TB),
        cc.reshape(NB, TB),
    )
    return f.reshape(CELLS), g.reshape(CELLS), gs, gt


def solution(mesh):
    placed = (
        P("row", None),
        P("col", None),
        P("row"),
        P("col"),
        P("row", "col", None),
        P("row", "col", None),
        P("row", "col"),
        P("row"),
        P("col"),
    )
    return jax.shard_map(
        on_device,
        mesh=mesh,
        in_specs=placed,
        out_specs=(P("row"), P("col"), P(("row", "col"), None), P(("col", "row"), None)),
        check_vma=False,
    )
```

```python
import jax
import jax.numpy as jnp
from jax import lax
from jax.experimental import pallas as pl
from jax.experimental.pallas import tpu as pltpu
from jax.sharding import PartitionSpec as P

MESH = pl.DeviceIdType.MESH
TB = 128
NB = 16
CELLS = NB * TB
E = 256
ROUNDS = 11
TALL = 8
HALF = TB // 2
SUBS = 2
SUB = E // SUBS
MASKED = -1e30
F32 = jnp.float32
BF16 = jnp.bfloat16
SHRINK = 2.0**-40
GROW = 2.0**40


def nt_dot(x, y):
    return lax.dot_general(x, y, (((1,), (1,)), ((), ())), preferred_element_type=F32)


def tn_dot(x, y):
    return lax.dot_general(x, y, (((0,), (0,)), ((), ())), preferred_element_type=F32)


def block(index, size=TB):
    return pl.ds(pl.multiple_of(index * size, size), size)


def kernel(
    src, tgt, a_ref, b_ref, rows_ref, cols_ref, count_ref, rc_ref, cc_ref,
    f_out, g_out, gs_out, gt_out,
    q, most, w, w_cols, part, land, wide, wide2, bias, vec, vec_w, srct, xs, ys, xb, yb, xt,
    gs_sum, gs_last, gs_land, gs_mid, gs_land2, gt_part, gt_sib, gt_sum, gt_land,
    ar_send, ar_recv, gs_ssem, gs_rsem, gs_ssem2, gs_rsem2, sib_ssem, sib_rsem, gt_ssem, gt_rsem,
):
    row_me = lax.axis_index("row")
    col_me = lax.axis_index("col")
    z_me = row_me // 2
    core = row_me % 2
    y_me = col_me // 4
    x_me = col_me % 4

    barrier = pltpu.get_barrier_semaphore()

    @pl.loop(1, NB)
    def _(k):
        pl.semaphore_signal(
            barrier, inc=1, device_id={"row": lax.rem(row_me + k, NB)}, device_id_type=MESH
        )
        pl.semaphore_signal(
            barrier, inc=1, device_id={"col": lax.rem(col_me + k, NB)}, device_id_type=MESH
        )

    eye = lax.broadcasted_iota(jnp.int32, (TB, TB), 0) == lax.broadcasted_iota(
        jnp.int32, (TB, TB), 1
    )

    def to_row(column):
        return jnp.sum(jnp.where(eye, column, 0.0), axis=0, keepdims=True)

    def to_column(row):
        return jnp.sum(jnp.where(eye, row, 0.0), axis=1, keepdims=True)

    def widen(value):
        vec[...] = value
        for rb in range(NB):
            wide[rb * TB : (rb + 1) * TB, :] = jnp.broadcast_to(
                to_column(vec[rb : rb + 1, :]), (TB, TB)
            )

    slot = lax.broadcasted_iota(jnp.int32, (TB, TB), 1)
    which = lax.broadcasted_iota(jnp.int32, (TB, TB), 0)
    live = slot < count_ref[...]
    row_hot = jnp.where((rows_ref[...] == which) & live, 1.0, 0.0).astype(BF16)
    col_hot = jnp.where((cols_ref[...] == which) & live, 1.0, 0.0).astype(BF16)
    present = nt_dot(row_hot[:NB], col_hot).astype(BF16)
    for cb in range(NB):
        spread = jnp.where(which == cb, 1.0, 0.0).astype(BF16)
        hits = jnp.dot(present, spread, preferred_element_type=F32)
        bias[:, cb * TB : (cb + 1) * TB] = jnp.where(hits > 0.5, 0.0, MASKED)

    @pl.loop(0, NB // TALL)
    def _(k):
        left = src[block(k, TALL * TB), :]
        for cb in range(NB // 2):
            at = slice(cb * 2 * TB, (cb + 1) * 2 * TB)
            s = nt_dot(left, tgt[at, :])
            for i in range(TALL):
                line = bias[pl.ds(k * TALL + i, 1), at]
                q[block(k * TALL + i), at] = s[i * TB : (i + 1) * TB] + line

    @pl.loop(0, NB)
    def _(rb):
        here = block(rb)
        top = q[here, 0:TB]
        for cb in range(1, NB):
            top = jnp.maximum(top, q[here, cb * TB : (cb + 1) * TB])
        total = jnp.exp(q[here, 0:TB] - top)
        for cb in range(1, NB):
            total += jnp.exp(q[here, cb * TB : (cb + 1) * TB] - top)
        wide[here, :] = top
        wide2[here, :] = total

    for rb in range(NB):
        here = slice(rb * TB, (rb + 1) * TB)
        top = wide[here, :]
        largest = jnp.max(top, axis=1, keepdims=True)
        total = jnp.sum(wide2[here, :] * jnp.exp(top - largest), axis=1, keepdims=True)
        part[0, rb : rb + 1, :] = to_row(largest + jnp.log(total))

    pl.semaphore_wait(barrier, 2 * (NB - 1))

    def start_reduce(index, axis):
        me = row_me if axis == "row" else col_me

        def send(k, carry):
            if axis == "row":
                j = k // 2
                far = lax.rem(4 + (1 - 2 * (j % 2)) * ((j + 1) // 2), 8)
                peer = lax.rem(z_me + far, 8) * 2 + lax.rem(core + 1 + k, 2)
            else:
                j = k // 4
                dy = lax.rem(2 + (1 - 2 * (j % 2)) * ((j + 1) // 2), 4)
                i = k % 4
                dx = lax.rem(2 + (1 - 2 * (i % 2)) * ((i + 1) // 2), 4)
                peer = lax.rem(y_me + dy, 4) * 4 + lax.rem(x_me + dx, 4)
            pltpu.make_async_remote_copy(
                src_ref=part.at[index],
                dst_ref=land.at[index, me],
                send_sem=ar_send.at[index],
                recv_sem=ar_recv.at[index],
                device_id={axis: peer},
                device_id_type=MESH,
            ).start()
            return carry

        lax.fori_loop(0, NB - 1, send, 0, unroll=True)
        land[index, me] = part[index]

    def end_reduce(index):
        others = land.at[index, pl.ds(0, NB - 1)]
        pltpu.make_async_copy(others, others, ar_recv.at[index]).wait()

    def summed(index):
        end_reduce(index)
        terms = [land[index, k] for k in range(NB)]
        while len(terms) > 1:
            terms = [terms[k] + terms[k + 1] for k in range(0, len(terms), 2)]
        return terms[0]

    def log_summed(index):
        end_reduce(index)
        largest = land[index, 0]
        for k in range(1, NB):
            largest = jnp.maximum(largest, land[index, k])
        total = jnp.exp(land[index, 0] - largest)
        for k in range(1, NB):
            total += jnp.exp(land[index, k] - largest)
        return largest + jnp.log(total)

    def row_pass(weights, index):
        vec_w[...] = weights

        @pl.loop(0, NB)
        def _(rb):
            here = block(rb)
            total = q[here, 0:TB] * vec_w[0:1, :]
            for cb in range(1, NB):
                total += q[here, cb * TB : (cb + 1) * TB] * vec_w[cb : cb + 1, :]
            wide[here, :] = total

        for rb in range(NB):
            total = jnp.sum(wide[rb * TB : (rb + 1) * TB, :], axis=1, keepdims=True)
            part[index, rb : rb + 1, :] = to_row(total)
        start_reduce(index, "col")

    def fold(value):
        total = value[0:8]
        for k in range(1, NB):
            total += value[k * 8 : (k + 1) * 8]
        return total

    def col_pass(weights, scale, index):
        widen(weights)

        def body(rb, totals):
            here = block(rb)
            u = wide[here, :]
            return tuple(
                totals[cb] + fold(q[here, cb * TB : (cb + 1) * TB] * u) for cb in range(NB)
            )

        totals = lax.fori_loop(0, NB, body, (jnp.zeros((8, TB), F32),) * NB)
        for cb in range(NB):
            vec[cb : cb + 1, :] = jnp.sum(totals[cb], axis=0, keepdims=True)
        part[index] = vec[...] * scale
        start_reduce(index, "row")

    start_reduce(0, "col")
    unit = jnp.where(
        lax.broadcasted_iota(jnp.int32, (E, E), 0) == lax.broadcasted_iota(jnp.int32, (E, E), 1),
        1.0,
        0.0,
    ).astype(BF16)
    for cb in range(NB // 2):
        at = slice(cb * 2 * TB, (cb + 1) * 2 * TB)
        srct[:, at] = nt_dot(unit, src[at, :]).astype(BF16)
    a = a_ref[...]
    b = b_ref[...]
    f1 = a - log_summed(0)

    widen(f1)

    def top_body(rb, tops):
        here = block(rb)
        u = wide[here, :]
        out = []
        for cb in range(NB):
            moved = q[here, cb * TB : (cb + 1) * TB] + u
            top = tops[cb]
            for k in range(NB):
                top = jnp.maximum(top, moved[k * 8 : (k + 1) * 8])
            out.append(top)
        return tuple(out)

    tops = lax.fori_loop(0, NB, top_body, (jnp.full((8, TB), MASKED, F32),) * NB)
    for cb in range(NB):
        vec_w[cb : cb + 1, :] = jnp.max(tops[cb], axis=0, keepdims=True)
    c = vec_w[...]

    def exp_body(rb, totals):
        here = block(rb)
        u = wide[here, :]
        out = []
        for cb in range(NB):
            at = slice(cb * TB, (cb + 1) * TB)
            value = jnp.exp((q[here, at] + u) - vec_w[cb : cb + 1, :])
            q[here, at] = value
            out.append(totals[cb] + fold(value))
        return tuple(out)

    totals = lax.fori_loop(0, NB, exp_body, (jnp.zeros((8, TB), F32),) * NB)
    for cb in range(NB):
        vec[cb : cb + 1, :] = jnp.sum(totals[cb], axis=0, keepdims=True)
    part[1] = c + jnp.log(vec[...])
    start_reduce(1, "row")
    exp_a = jnp.exp(a)
    exp_b = jnp.exp(b)
    inv_a = jnp.exp(-a)
    inv_b = jnp.exp(-b)
    g1 = b - log_summed(1)

    d = jnp.exp(c + g1)

    def put(ref, term, value):
        vec[...] = value
        for k in range(NB):
            ref[k * 8 + term : k * 8 + term + 1, :] = vec[k : k + 1, :]

    xs[...] = jnp.zeros_like(xs)
    ys[...] = jnp.zeros_like(ys)

    def thirds(value):
        first = value.astype(BF16).astype(F32)
        rest = value - first
        second = rest.astype(BF16).astype(F32)
        third = (rest - second).astype(BF16).astype(F32)
        return first, second, third

    def stacked(ref, to, order):
        for k in range(NB):
            parts = thirds(ref[k * 8 : (k + 1) * 8, :])
            to[:, k * TB : (k + 1) * TB] = jnp.concatenate(
                [parts[i] for i in order], axis=0
            ).astype(BF16)

    def stack_x():
        stacked(xs, xb, (0, 0, 1, 0, 2, 1))
        for k in range(NB // 2):
            at = slice(k * 2 * TB, (k + 1) * 2 * TB)
            xt[at, :] = nt_dot(unit, xb[:, at]).astype(BF16)

    def stack_y():
        stacked(ys, yb, (0, 1, 0, 2, 0, 1))

    def source_product(into, line, with_most):
        vec_w[...] = line

        @pl.loop(0, NB // TALL)
        def _(k):
            here = block(k, TALL * TB)
            for cb in range(NB):
                col = slice(cb * TB, (cb + 1) * TB)
                value = q[here, col] * vec_w[cb : cb + 1, :]
                if with_most:
                    value += most[here, col]
                w[:, col] = value.astype(BF16)
            into[here, :] = jnp.dot(w[...], tgt[...], preferred_element_type=F32)

    last_line = jnp.exp(c) * -SHRINK
    row_pass(d, 2)
    put(ys, 4, d * -SHRINK)
    u2 = exp_a / summed(2)
    col_pass(u2, d, 3)
    put(xs, 1, u2)
    source_product(gs_last, last_line, False)
    v2 = exp_b / summed(3)
    dv2 = d * v2
    row_pass(dv2, 4)
    put(ys, 3, dv2 * -SHRINK)
    u3 = exp_a / summed(4)
    col_pass(u3, d, 5)
    put(xs, 0, u3)
    f_out[...] = f1 + jnp.log(u3)
    v3 = exp_b / summed(5)

    y3 = d * v3 * inv_b * cc_ref[...]
    row_pass(y3, 6)
    put(ys, 0, y3 * -SHRINK)
    g_out[...] = g1 + jnp.log(v3)
    x3 = u3 * inv_a * (rc_ref[...] - u3 * summed(6))
    col_pass(x3, d, 7)
    put(xs, 3, x3)
    y2 = dv2 * inv_b * (-v2 * summed(7))
    row_pass(y2, 8)
    put(ys, 1, y2 * -SHRINK)
    x2 = u2 * inv_a * (-u2 * summed(8))
    col_pass(x2, d, 9)
    put(xs, 4, x2)
    stack_x()
    stack_y()

    @pl.loop(0, NB // TALL)
    def _(k):
        here = block(k, TALL * TB)
        for cb in range(NB // 2):
            at = slice(cb * 2 * TB, (cb + 1) * 2 * TB)
            factor = jnp.dot(xt[here, :], yb[:, at], preferred_element_type=F32)
            most[here, at] = q[here, at] * factor

    y1 = d * inv_b * -summed(9)
    row_pass(y1, 10)
    source_product(gs_sum, y1 * -SHRINK, True)
    x1 = inv_a * -summed(10)

    widen(x1)

    def first_copy(half, other, k):
        if half == 0:
            to_x = lax.rem(x_me + k, 4)
            owner, peer = other * 4 + to_x, y_me * 4 + to_x
        else:
            to_y = lax.rem(y_me + k, 4)
            owner, peer = to_y * 4 + other, to_y * 4 + x_me
        rows = pl.ds(pl.multiple_of(owner * TB + half * HALF, HALF), HALF)
        return pltpu.make_async_remote_copy(
            src_ref=gs_sum.at[rows],
            dst_ref=gs_land.at[half, other, x_me if half == 0 else y_me],
            send_sem=gs_ssem.at[half],
            recv_sem=gs_rsem.at[half, other],
            device_id={"col": peer},
            device_id_type=MESH,
        )

    def other_at(half, k):
        return lax.rem((y_me if half == 0 else x_me) + 2 + (1 - 2 * (k % 2)) * ((k + 1) // 2), 4)

    def second_stage(k):
        for half in range(2):
            other = other_at(half, k)
            others = gs_land.at[half, other, pl.ds(0, 3)]
            pltpu.make_async_copy(others, others, gs_rsem.at[half, other]).wait()
            mine = x_me if half == 0 else y_me
            owner = other * 4 + x_me if half == 0 else y_me * 4 + other
            rows = pl.ds(pl.multiple_of(owner * TB + half * HALF, HALF), HALF)
            total = gs_sum[rows, :]
            for far in range(1, 4):
                total += gs_land[half, other, lax.rem(mine + far, 4)]
            gs_mid[half, other] = total

            @pl.when(k < 3)
            def _():
                peer = other * 4 + x_me if half == 0 else y_me * 4 + other
                pltpu.make_async_remote_copy(
                    src_ref=gs_mid.at[half, other],
                    dst_ref=gs_land2.at[half, y_me if half == 0 else x_me],
                    send_sem=gs_ssem2.at[half],
                    recv_sem=gs_rsem2.at[half],
                    device_id={"col": peer},
                    device_id_type=MESH,
                ).start()

    def first_stage():
        @pl.loop(0, NB)
        def _(rb):
            here = block(rb)
            u = wide[here, :]
            for half in range(2):
                at = slice(half * TB, (half + 1) * TB)
                gs_sum[here, at] += u * gs_last[here, at]

        @pl.loop(0, 4)
        def _(k):
            for half in range(2):
                for far in (2, 1, 3):
                    first_copy(half, other_at(half, k), far).start()

    vec_w[...] = last_line
    vec[...] = y1 * -SHRINK

    def chip_at(k):
        return lax.rem(z_me + 4 + (1 - 2 * (k % 2)) * ((k + 1) // 2), 8)

    def sibling_copy(j):
        return pltpu.make_async_remote_copy(
            src_ref=gt_part.at[j, 1 - core],
            dst_ref=gt_sib.at[j],
            send_sem=sib_ssem.at[j],
            recv_sem=sib_rsem.at[j],
            device_id={"row": z_me * 2 + 1 - core},
            device_id_type=MESH,
        )

    def ring_copy(way, step, sub):
        j = lax.rem(z_me + jnp.where(way == 0, 4 - step, 4 + step), 8)
        rows = pl.ds(sub * SUB, SUB)
        peer = lax.rem(z_me + jnp.where(way == 0, 1, 7), 8)
        return pltpu.make_async_remote_copy(
            src_ref=gt_sum.at[j, rows],
            dst_ref=gt_land.at[way, step, rows],
            send_sem=gt_ssem.at[way, step, sub],
            recv_sem=gt_rsem.at[way, step, sub],
            device_id={"row": peer * 2 + core},
            device_id_type=MESH,
        )

    def ready(k):
        j = chip_at(k)
        sibling_copy(j).wait_recv()
        gt_sum[j] = gt_part[j, core] + gt_sib[j]

    def advance(k):
        ready(k)
        j = chip_at(k)
        way = (k + 1) % 2
        step = (k + 1) // 2
        for sub in range(SUBS):
            rows = pl.ds(sub * SUB, SUB)

            @pl.when((step > 1) | (way == sub // (SUBS // 2)))
            def _():
                ring_copy(way, step - 1, sub).wait_recv()
                gt_sum[j, rows] += gt_land[way, step - 1, rows]

            ring_copy(way, step, sub).start()

    @pl.loop(0, 8)
    def _(k):
        j = chip_at(k)
        cols = block(j, 2 * TB)
        for part_k in range(NB // 2):
            here = slice(part_k * 2 * TB, (part_k + 1) * 2 * TB)
            u = wide[here, :]
            for half in range(2):
                col = block(j * 2 + half)
                last = vec_w[pl.ds(j * 2 + half, 1), :]
                line = vec[pl.ds(j * 2 + half, 1), :]
                value = most[here, col] + q[here, col] * (line + u * last)
                w_cols[here, half * TB : (half + 1) * TB] = value.astype(BF16)
        total = jnp.dot(srct[...], w_cols[...], preferred_element_type=F32)
        gt_part[j, 0] = total[:, :TB]
        gt_part[j, 1] = total[:, TB:]
        sibling_copy(j).start()

        @pl.when(k == 0)
        def _():
            first_stage()

        @pl.when(k == 1)
        def _():
            ready(0)
            for sub in range(SUBS):
                ring_copy(sub // (SUBS // 2), 0, sub).start()

        @pl.when(k > 1)
        def _():
            advance(k - 1)

        @pl.when(k > 4)
        def _():
            second_stage(k - 5)

    ready(7)
    second_stage(3)

    for way in range(2):
        for sub in range(SUBS):
            ring_copy(way, 3, sub).wait_recv()
    for k in range(2):
        at = slice(k * TB, (k + 1) * TB)
        total = gt_sum[z_me, at, :] + gt_land[0, 3, at, :] + gt_land[1, 3, at, :]
        gt_out[:, at] = (total * GROW).T

    for half in range(2):
        others = gs_land2.at[half, pl.ds(0, 3)]
        pltpu.make_async_copy(others, others, gs_rsem2.at[half]).wait()
        mine = y_me if half == 0 else x_me
        total = gs_mid[half, mine]
        for far in range(1, 4):
            total += gs_land2[half, lax.rem(mine + far, 4)]
        gs_out[half * HALF : (half + 1) * HALF, :] = total * GROW

    @pl.loop(0, ROUNDS)
    def _(index):
        others = land.at[index, pl.ds(0, NB - 1)]
        pltpu.make_async_copy(others, others, ar_send.at[index]).wait()

    for half in range(2):
        others = gs_land.at[half, pl.ds(0, 3)]
        pltpu.make_async_copy(others, others, gs_ssem.at[half]).wait()
        others = gs_land2.at[half, pl.ds(0, 3)]
        pltpu.make_async_copy(others, others, gs_ssem2.at[half]).wait()

    @pl.loop(0, 8)
    def _(j):
        sibling_copy(j).wait_send()

    for sub in range(SUBS):
        ring_copy(sub // (SUBS // 2), 0, sub).wait_send()
        for way in range(2):
            for step in range(1, 4):
                ring_copy(way, step, sub).wait_send()


def on_device(src, tgt, a, b, rows, cols, counts, rc, cc):
    vmem = pl.BlockSpec(memory_space=pltpu.VMEM)
    dma = pltpu.SemaphoreType.DMA
    f, g, gs, gt = pl.pallas_call(
        kernel,
        out_shape=(
            jax.ShapeDtypeStruct((NB, TB), F32),
            jax.ShapeDtypeStruct((NB, TB), F32),
            jax.ShapeDtypeStruct((TB, E), F32),
            jax.ShapeDtypeStruct((TB, E), F32),
        ),
        in_specs=[vmem] * 9,
        out_specs=(vmem,) * 4,
        scratch_shapes=[
            pltpu.VMEM((CELLS, CELLS), F32),
            pltpu.VMEM((CELLS, CELLS), F32),
            pltpu.VMEM((TALL * TB, CELLS), BF16),
            pltpu.VMEM((CELLS, 2 * TB), BF16),
            pltpu.VMEM((ROUNDS, NB, TB), F32),
            pltpu.VMEM((ROUNDS, NB, NB, TB), F32),
            pltpu.VMEM((CELLS, TB), F32),
            pltpu.VMEM((CELLS, TB), F32),
            pltpu.VMEM((NB, CELLS), F32),
            pltpu.VMEM((NB, TB), F32),
            pltpu.VMEM((NB, TB), F32),
            pltpu.VMEM((E, CELLS), BF16),
            pltpu.VMEM((NB * 8, TB), F32),
            pltpu.VMEM((NB * 8, TB), F32),
            pltpu.VMEM((48, CELLS), BF16),
            pltpu.VMEM((48, CELLS), BF16),
            pltpu.VMEM((CELLS, 48), BF16),
            pltpu.VMEM((CELLS, E), F32),
            pltpu.VMEM((CELLS, E), F32),
            pltpu.VMEM((2, 4, 4, HALF, E), F32),
            pltpu.VMEM((2, 4, HALF, E), F32),
            pltpu.VMEM((2, 4, HALF, E), F32),
            pltpu.VMEM((8, 2, E, TB), F32),
            pltpu.VMEM((8, E, TB), F32),
            pltpu.VMEM((8, E, TB), F32),
            pltpu.VMEM((2, 4, E, TB), F32),
            dma((ROUNDS,)),
            dma((ROUNDS,)),
            dma((2,)),
            dma((2, 4)),
            dma((2,)),
            dma((2,)),
            dma((8,)),
            dma((8,)),
            dma((2, 4, SUBS)),
            dma((2, 4, SUBS)),
        ],
        compiler_params=pltpu.CompilerParams(
            collective_id=0, has_side_effects=True, vmem_limit_bytes=60 << 20
        ),
    )(
        src,
        tgt,
        a.reshape(NB, TB),
        b.reshape(NB, TB),
        rows.reshape(1, TB),
        cols.reshape(1, TB),
        counts,
        rc.reshape(NB, TB),
        cc.reshape(NB, TB),
    )
    return f.reshape(CELLS), g.reshape(CELLS), gs, gt


def solution(mesh):
    placed = (
        P("row", None),
        P("col", None),
        P("row"),
        P("col"),
        P("row", "col", None),
        P("row", "col", None),
        P("row", "col"),
        P("row"),
        P("col"),
    )
    return jax.shard_map(
        on_device,
        mesh=mesh,
        in_specs=placed,
        out_specs=(P("row"), P("col"), P(("row", "col"), None), P(("col", "row"), None)),
        check_vma=False,
    )
```

```python
import jax
import jax.numpy as jnp
from jax import lax
from jax.experimental import pallas as pl
from jax.experimental.pallas import tpu as pltpu
from jax.sharding import PartitionSpec as P

MESH = pl.DeviceIdType.MESH
TB = 128
NB = 16
CELLS = NB * TB
E = 256
ROUNDS = 11
TALL = 8
HALF = TB // 2
SUBS = 2
SUB = E // SUBS
MASKED = -1e30
F32 = jnp.float32
BF16 = jnp.bfloat16
SHRINK = 2.0**-40
GROW = 2.0**40


def nt_dot(x, y):
    return lax.dot_general(x, y, (((1,), (1,)), ((), ())), preferred_element_type=F32)


def tn_dot(x, y):
    return lax.dot_general(x, y, (((0,), (0,)), ((), ())), preferred_element_type=F32)


def block(index, size=TB):
    return pl.ds(pl.multiple_of(index * size, size), size)


def kernel(
    src, tgt, a_ref, b_ref, rows_ref, cols_ref, count_ref, rc_ref, cc_ref,
    f_out, g_out, gs_out, gt_out,
    q, most, w, w_cols, part, land, wide, wide2, bias, vec, vec_w, srct, xs, ys, xb, yb, xt,
    gs_sum, gs_last, gs_land, gs_mid, gs_land2, gt_part, gt_sib, gt_sum, gt_land,
    ar_send, ar_recv, gs_ssem, gs_rsem, gs_ssem2, gs_rsem2, sib_ssem, sib_rsem, gt_ssem, gt_rsem,
):
    row_me = lax.axis_index("row")
    col_me = lax.axis_index("col")
    z_me = row_me // 2
    core = row_me % 2
    y_me = col_me // 4
    x_me = col_me % 4

    barrier = pltpu.get_barrier_semaphore()

    @pl.loop(1, NB)
    def _(k):
        pl.semaphore_signal(
            barrier, inc=1, device_id={"row": lax.rem(row_me + k, NB)}, device_id_type=MESH
        )
        pl.semaphore_signal(
            barrier, inc=1, device_id={"col": lax.rem(col_me + k, NB)}, device_id_type=MESH
        )

    eye = lax.broadcasted_iota(jnp.int32, (TB, TB), 0) == lax.broadcasted_iota(
        jnp.int32, (TB, TB), 1
    )

    def to_row(column):
        return jnp.sum(jnp.where(eye, column, 0.0), axis=0, keepdims=True)

    def to_column(row):
        return jnp.sum(jnp.where(eye, row, 0.0), axis=1, keepdims=True)

    def widen(value):
        vec[...] = value
        for rb in range(NB):
            wide[rb * TB : (rb + 1) * TB, :] = jnp.broadcast_to(
                to_column(vec[rb : rb + 1, :]), (TB, TB)
            )

    slot = lax.broadcasted_iota(jnp.int32, (TB, TB), 1)
    which = lax.broadcasted_iota(jnp.int32, (TB, TB), 0)
    live = slot < count_ref[...]
    row_hot = jnp.where((rows_ref[...] == which) & live, 1.0, 0.0).astype(BF16)
    col_hot = jnp.where((cols_ref[...] == which) & live, 1.0, 0.0).astype(BF16)
    present = nt_dot(row_hot[:NB], col_hot).astype(BF16)
    for cb in range(NB):
        spread = jnp.where(which == cb, 1.0, 0.0).astype(BF16)
        hits = jnp.dot(present, spread, preferred_element_type=F32)
        bias[:, cb * TB : (cb + 1) * TB] = jnp.where(hits > 0.5, 0.0, MASKED)

    @pl.loop(0, NB // TALL)
    def _(k):
        left = src[block(k, TALL * TB), :]
        for cb in range(NB // 2):
            at = slice(cb * 2 * TB, (cb + 1) * 2 * TB)
            s = nt_dot(left, tgt[at, :])
            for i in range(TALL):
                line = bias[pl.ds(k * TALL + i, 1), at]
                q[block(k * TALL + i), at] = s[i * TB : (i + 1) * TB] + line

    @pl.loop(0, NB)
    def _(rb):
        here = block(rb)
        top = q[here, 0:TB]
        for cb in range(1, NB):
            top = jnp.maximum(top, q[here, cb * TB : (cb + 1) * TB])
        total = jnp.exp(q[here, 0:TB] - top)
        for cb in range(1, NB):
            total += jnp.exp(q[here, cb * TB : (cb + 1) * TB] - top)
        wide[here, :] = top
        wide2[here, :] = total

    for rb in range(NB):
        here = slice(rb * TB, (rb + 1) * TB)
        top = wide[here, :]
        largest = jnp.max(top, axis=1, keepdims=True)
        total = jnp.sum(wide2[here, :] * jnp.exp(top - largest), axis=1, keepdims=True)
        part[0, rb : rb + 1, :] = to_row(largest + jnp.log(total))

    pl.semaphore_wait(barrier, 2 * (NB - 1))

    def start_reduce(index, axis):
        me = row_me if axis == "row" else col_me

        def send(k, carry):
            if axis == "row":
                j = k // 2
                far = lax.rem(4 + (1 - 2 * (j % 2)) * ((j + 1) // 2), 8)
                peer = lax.rem(z_me + far, 8) * 2 + lax.rem(core + 1 + k, 2)
            else:
                j = k // 4
                dy = lax.rem(2 + (1 - 2 * (j % 2)) * ((j + 1) // 2), 4)
                i = k % 4
                dx = lax.rem(2 + (1 - 2 * (i % 2)) * ((i + 1) // 2), 4)
                peer = lax.rem(y_me + dy, 4) * 4 + lax.rem(x_me + dx, 4)
            pltpu.make_async_remote_copy(
                src_ref=part.at[index],
                dst_ref=land.at[index, me],
                send_sem=ar_send.at[index],
                recv_sem=ar_recv.at[index],
                device_id={axis: peer},
                device_id_type=MESH,
            ).start()
            return carry

        lax.fori_loop(0, NB - 1, send, 0, unroll=True)
        land[index, me] = part[index]

    def end_reduce(index):
        others = land.at[index, pl.ds(0, NB - 1)]
        pltpu.make_async_copy(others, others, ar_recv.at[index]).wait()

    def summed(index):
        end_reduce(index)
        terms = [land[index, k] for k in range(NB)]
        while len(terms) > 1:
            terms = [terms[k] + terms[k + 1] for k in range(0, len(terms), 2)]
        return terms[0]

    def log_summed(index):
        end_reduce(index)
        largest = land[index, 0]
        for k in range(1, NB):
            largest = jnp.maximum(largest, land[index, k])
        total = jnp.exp(land[index, 0] - largest)
        for k in range(1, NB):
            total += jnp.exp(land[index, k] - largest)
        return largest + jnp.log(total)

    def row_pass(weights, index):
        vec_w[...] = weights

        @pl.loop(0, NB)
        def _(rb):
            here = block(rb)
            total = q[here, 0:TB] * vec_w[0:1, :]
            for cb in range(1, NB):
                total += q[here, cb * TB : (cb + 1) * TB] * vec_w[cb : cb + 1, :]
            wide[here, :] = total

        for rb in range(NB):
            total = jnp.sum(wide[rb * TB : (rb + 1) * TB, :], axis=1, keepdims=True)
            part[index, rb : rb + 1, :] = to_row(total)
        start_reduce(index, "col")

    def fold(value):
        total = value[0:8]
        for k in range(1, NB):
            total += value[k * 8 : (k + 1) * 8]
        return total

    def col_pass(weights, scale, index):
        widen(weights)

        def body(rb, totals):
            here = block(rb)
            u = wide[here, :]
            return tuple(
                totals[cb] + fold(q[here, cb * TB : (cb + 1) * TB] * u) for cb in range(NB)
            )

        totals = lax.fori_loop(0, NB, body, (jnp.zeros((8, TB), F32),) * NB)
        for cb in range(NB):
            vec[cb : cb + 1, :] = jnp.sum(totals[cb], axis=0, keepdims=True)
        part[index] = vec[...] * scale
        start_reduce(index, "row")

    start_reduce(0, "col")
    unit = jnp.where(
        lax.broadcasted_iota(jnp.int32, (E, E), 0) == lax.broadcasted_iota(jnp.int32, (E, E), 1),
        1.0,
        0.0,
    ).astype(BF16)
    for cb in range(NB // 2):
        at = slice(cb * 2 * TB, (cb + 1) * 2 * TB)
        srct[:, at] = nt_dot(unit, src[at, :]).astype(BF16)
    a = a_ref[...]
    b = b_ref[...]
    f1 = a - log_summed(0)

    widen(f1)

    def top_body(rb, tops):
        here = block(rb)
        u = wide[here, :]
        out = []
        for cb in range(NB):
            moved = q[here, cb * TB : (cb + 1) * TB] + u
            top = tops[cb]
            for k in range(NB):
                top = jnp.maximum(top, moved[k * 8 : (k + 1) * 8])
            out.append(top)
        return tuple(out)

    tops = lax.fori_loop(0, NB, top_body, (jnp.full((8, TB), MASKED, F32),) * NB)
    for cb in range(NB):
        vec_w[cb : cb + 1, :] = jnp.max(tops[cb], axis=0, keepdims=True)
    c = vec_w[...]

    def exp_body(rb, totals):
        here = block(rb)
        u = wide[here, :]
        out = []
        for cb in range(NB):
            at = slice(cb * TB, (cb + 1) * TB)
            value = jnp.exp((q[here, at] + u) - vec_w[cb : cb + 1, :])
            q[here, at] = value
            out.append(totals[cb] + fold(value))
        return tuple(out)

    totals = lax.fori_loop(0, NB, exp_body, (jnp.zeros((8, TB), F32),) * NB)
    for cb in range(NB):
        vec[cb : cb + 1, :] = jnp.sum(totals[cb], axis=0, keepdims=True)
    part[1] = c + jnp.log(vec[...])
    start_reduce(1, "row")
    exp_a = jnp.exp(a)
    exp_b = jnp.exp(b)
    inv_a = jnp.exp(-a)
    inv_b = jnp.exp(-b)
    g1 = b - log_summed(1)

    d = jnp.exp(c + g1)

    def put(ref, term, value):
        vec[...] = value
        for k in range(NB):
            ref[k * 8 + term : k * 8 + term + 1, :] = vec[k : k + 1, :]

    xs[...] = jnp.zeros_like(xs)
    ys[...] = jnp.zeros_like(ys)

    def thirds(value):
        first = value.astype(BF16).astype(F32)
        rest = value - first
        second = rest.astype(BF16).astype(F32)
        third = (rest - second).astype(BF16).astype(F32)
        return first, second, third

    def stacked(ref, to, order):
        for k in range(NB):
            parts = thirds(ref[k * 8 : (k + 1) * 8, :])
            to[:, k * TB : (k + 1) * TB] = jnp.concatenate(
                [parts[i] for i in order], axis=0
            ).astype(BF16)

    def stack_x():
        stacked(xs, xb, (0, 0, 1, 0, 2, 1))
        for k in range(NB // 2):
            at = slice(k * 2 * TB, (k + 1) * 2 * TB)
            xt[at, :] = nt_dot(unit, xb[:, at]).astype(BF16)

    def stack_y():
        stacked(ys, yb, (0, 1, 0, 2, 0, 1))

    def source_product(into, line, with_most):
        vec_w[...] = line

        @pl.loop(0, NB // TALL)
        def _(k):
            here = block(k, TALL * TB)
            for cb in range(NB):
                col = slice(cb * TB, (cb + 1) * TB)
                value = q[here, col] * vec_w[cb : cb + 1, :]
                if with_most:
                    value += most[here, col]
                w[:, col] = value.astype(BF16)
            into[here, :] = jnp.dot(w[...], tgt[...], preferred_element_type=F32)

    last_line = jnp.exp(c) * -SHRINK
    row_pass(d, 2)
    put(ys, 4, d * -SHRINK)
    u2 = exp_a / summed(2)
    col_pass(u2, d, 3)
    put(xs, 1, u2)
    source_product(gs_last, last_line, False)
    v2 = exp_b / summed(3)
    dv2 = d * v2
    row_pass(dv2, 4)
    put(ys, 3, dv2 * -SHRINK)
    u3 = exp_a / summed(4)
    col_pass(u3, d, 5)
    put(xs, 0, u3)
    f_out[...] = -(f1 + jnp.log(u3))
    v3 = exp_b / summed(5)

    y3 = d * v3 * inv_b * cc_ref[...]
    row_pass(y3, 6)
    put(ys, 0, y3 * -SHRINK)
    g_out[...] = -(g1 + jnp.log(v3))
    x3 = u3 * inv_a * (rc_ref[...] - u3 * summed(6))
    col_pass(x3, d, 7)
    put(xs, 3, x3)
    y2 = dv2 * inv_b * (-v2 * summed(7))
    row_pass(y2, 8)
    put(ys, 1, y2 * -SHRINK)
    x2 = u2 * inv_a * (-u2 * summed(8))
    col_pass(x2, d, 9)
    put(xs, 4, x2)
    stack_x()
    stack_y()

    @pl.loop(0, NB // TALL)
    def _(k):
        here = block(k, TALL * TB)
        for cb in range(NB // 2):
            at = slice(cb * 2 * TB, (cb + 1) * 2 * TB)
            factor = jnp.dot(xt[here, :], yb[:, at], preferred_element_type=F32)
            most[here, at] = q[here, at] * factor

    y1 = d * inv_b * -summed(9)
    row_pass(y1, 10)
    source_product(gs_sum, y1 * -SHRINK, True)
    x1 = inv_a * -summed(10)

    widen(x1)

    def first_copy(half, other, k):
        if half == 0:
            to_x = lax.rem(x_me + k, 4)
            owner, peer = other * 4 + to_x, y_me * 4 + to_x
        else:
            to_y = lax.rem(y_me + k, 4)
            owner, peer = to_y * 4 + other, to_y * 4 + x_me
        rows = pl.ds(pl.multiple_of(owner * TB + half * HALF, HALF), HALF)
        return pltpu.make_async_remote_copy(
            src_ref=gs_sum.at[rows],
            dst_ref=gs_land.at[half, other, x_me if half == 0 else y_me],
            send_sem=gs_ssem.at[half],
            recv_sem=gs_rsem.at[half, other],
            device_id={"col": peer},
            device_id_type=MESH,
        )

    def other_at(half, k):
        return lax.rem((y_me if half == 0 else x_me) + 2 + (1 - 2 * (k % 2)) * ((k + 1) // 2), 4)

    def second_stage(k):
        for half in range(2):
            other = other_at(half, k)
            others = gs_land.at[half, other, pl.ds(0, 3)]
            pltpu.make_async_copy(others, others, gs_rsem.at[half, other]).wait()
            mine = x_me if half == 0 else y_me
            owner = other * 4 + x_me if half == 0 else y_me * 4 + other
            rows = pl.ds(pl.multiple_of(owner * TB + half * HALF, HALF), HALF)
            total = gs_sum[rows, :]
            for far in range(1, 4):
                total += gs_land[half, other, lax.rem(mine + far, 4)]
            gs_mid[half, other] = total

            @pl.when(k < 3)
            def _():
                peer = other * 4 + x_me if half == 0 else y_me * 4 + other
                pltpu.make_async_remote_copy(
                    src_ref=gs_mid.at[half, other],
                    dst_ref=gs_land2.at[half, y_me if half == 0 else x_me],
                    send_sem=gs_ssem2.at[half],
                    recv_sem=gs_rsem2.at[half],
                    device_id={"col": peer},
                    device_id_type=MESH,
                ).start()

    def first_stage():
        @pl.loop(0, NB)
        def _(rb):
            here = block(rb)
            u = wide[here, :]
            for half in range(2):
                at = slice(half * TB, (half + 1) * TB)
                gs_sum[here, at] += u * gs_last[here, at]

        @pl.loop(0, 4)
        def _(k):
            for half in range(2):
                for far in (2, 1, 3):
                    first_copy(half, other_at(half, k), far).start()

    vec_w[...] = last_line
    vec[...] = y1 * -SHRINK

    def chip_at(k):
        return lax.rem(z_me + 4 + (1 - 2 * (k % 2)) * ((k + 1) // 2), 8)

    def sibling_copy(j):
        return pltpu.make_async_remote_copy(
            src_ref=gt_part.at[j, 1 - core],
            dst_ref=gt_sib.at[j],
            send_sem=sib_ssem.at[j],
            recv_sem=sib_rsem.at[j],
            device_id={"row": z_me * 2 + 1 - core},
            device_id_type=MESH,
        )

    def ring_copy(way, step, sub):
        j = lax.rem(z_me + jnp.where(way == 0, 4 - step, 4 + step), 8)
        rows = pl.ds(sub * SUB, SUB)
        peer = lax.rem(z_me + jnp.where(way == 0, 1, 7), 8)
        return pltpu.make_async_remote_copy(
            src_ref=gt_sum.at[j, rows],
            dst_ref=gt_land.at[way, step, rows],
            send_sem=gt_ssem.at[way, step, sub],
            recv_sem=gt_rsem.at[way, step, sub],
            device_id={"row": peer * 2 + core},
            device_id_type=MESH,
        )

    def ready(k):
        j = chip_at(k)
        sibling_copy(j).wait_recv()
        gt_sum[j] = gt_part[j, core] + gt_sib[j]

    def advance(k):
        ready(k)
        j = chip_at(k)
        way = (k + 1) % 2
        step = (k + 1) // 2
        for sub in range(SUBS):
            rows = pl.ds(sub * SUB, SUB)

            @pl.when((step > 1) | (way == sub // (SUBS // 2)))
            def _():
                ring_copy(way, step - 1, sub).wait_recv()
                gt_sum[j, rows] += gt_land[way, step - 1, rows]

            ring_copy(way, step, sub).start()

    @pl.loop(0, 8)
    def _(k):
        j = chip_at(k)
        cols = block(j, 2 * TB)
        for part_k in range(NB // 2):
            here = slice(part_k * 2 * TB, (part_k + 1) * 2 * TB)
            u = wide[here, :]
            for half in range(2):
                col = block(j * 2 + half)
                last = vec_w[pl.ds(j * 2 + half, 1), :]
                line = vec[pl.ds(j * 2 + half, 1), :]
                value = most[here, col] + q[here, col] * (line + u * last)
                w_cols[here, half * TB : (half + 1) * TB] = value.astype(BF16)
        total = jnp.dot(srct[...], w_cols[...], preferred_element_type=F32)
        gt_part[j, 0] = total[:, :TB]
        gt_part[j, 1] = total[:, TB:]
        sibling_copy(j).start()

        @pl.when(k == 0)
        def _():
            first_stage()

        @pl.when(k == 1)
        def _():
            ready(0)
            for sub in range(SUBS):
                ring_copy(sub // (SUBS // 2), 0, sub).start()

        @pl.when(k > 1)
        def _():
            advance(k - 1)

        @pl.when(k > 4)
        def _():
            second_stage(k - 5)

    ready(7)
    second_stage(3)

    for way in range(2):
        for sub in range(SUBS):
            ring_copy(way, 3, sub).wait_recv()
    for k in range(2):
        at = slice(k * TB, (k + 1) * TB)
        total = gt_sum[z_me, at, :] + gt_land[0, 3, at, :] + gt_land[1, 3, at, :]
        gt_out[:, at] = total.T

    for half in range(2):
        others = gs_land2.at[half, pl.ds(0, 3)]
        pltpu.make_async_copy(others, others, gs_rsem2.at[half]).wait()
        mine = y_me if half == 0 else x_me
        total = gs_mid[half, mine]
        for far in range(1, 4):
            total += gs_land2[half, lax.rem(mine + far, 4)]
        gs_out[half * HALF : (half + 1) * HALF, :] = total

    @pl.loop(0, ROUNDS)
    def _(index):
        others = land.at[index, pl.ds(0, NB - 1)]
        pltpu.make_async_copy(others, others, ar_send.at[index]).wait()

    for half in range(2):
        others = gs_land.at[half, pl.ds(0, 3)]
        pltpu.make_async_copy(others, others, gs_ssem.at[half]).wait()
        others = gs_land2.at[half, pl.ds(0, 3)]
        pltpu.make_async_copy(others, others, gs_ssem2.at[half]).wait()

    @pl.loop(0, 8)
    def _(j):
        sibling_copy(j).wait_send()

    for sub in range(SUBS):
        ring_copy(sub // (SUBS // 2), 0, sub).wait_send()
        for way in range(2):
            for step in range(1, 4):
                ring_copy(way, step, sub).wait_send()


def on_device(src, tgt, a, b, rows, cols, counts, rc, cc):
    vmem = pl.BlockSpec(memory_space=pltpu.VMEM)
    dma = pltpu.SemaphoreType.DMA
    f, g, gs, gt = pl.pallas_call(
        kernel,
        out_shape=(
            jax.ShapeDtypeStruct((NB, TB), F32),
            jax.ShapeDtypeStruct((NB, TB), F32),
            jax.ShapeDtypeStruct((TB, E), F32),
            jax.ShapeDtypeStruct((TB, E), F32),
        ),
        in_specs=[vmem] * 9,
        out_specs=(vmem,) * 4,
        scratch_shapes=[
            pltpu.VMEM((CELLS, CELLS), F32),
            pltpu.VMEM((CELLS, CELLS), F32),
            pltpu.VMEM((TALL * TB, CELLS), BF16),
            pltpu.VMEM((CELLS, 2 * TB), BF16),
            pltpu.VMEM((ROUNDS, NB, TB), F32),
            pltpu.VMEM((ROUNDS, NB, NB, TB), F32),
            pltpu.VMEM((CELLS, TB), F32),
            pltpu.VMEM((CELLS, TB), F32),
            pltpu.VMEM((NB, CELLS), F32),
            pltpu.VMEM((NB, TB), F32),
            pltpu.VMEM((NB, TB), F32),
            pltpu.VMEM((E, CELLS), BF16),
            pltpu.VMEM((NB * 8, TB), F32),
            pltpu.VMEM((NB * 8, TB), F32),
            pltpu.VMEM((48, CELLS), BF16),
            pltpu.VMEM((48, CELLS), BF16),
            pltpu.VMEM((CELLS, 48), BF16),
            pltpu.VMEM((CELLS, E), F32),
            pltpu.VMEM((CELLS, E), F32),
            pltpu.VMEM((2, 4, 4, HALF, E), F32),
            pltpu.VMEM((2, 4, HALF, E), F32),
            pltpu.VMEM((2, 4, HALF, E), F32),
            pltpu.VMEM((8, 2, E, TB), F32),
            pltpu.VMEM((8, E, TB), F32),
            pltpu.VMEM((8, E, TB), F32),
            pltpu.VMEM((2, 4, E, TB), F32),
            dma((ROUNDS,)),
            dma((ROUNDS,)),
            dma((2,)),
            dma((2, 4)),
            dma((2,)),
            dma((2,)),
            dma((8,)),
            dma((8,)),
            dma((2, 4, SUBS)),
            dma((2, 4, SUBS)),
        ],
        compiler_params=pltpu.CompilerParams(
            collective_id=0, has_side_effects=True, vmem_limit_bytes=60 << 20
        ),
    )(
        src,
        tgt,
        a.reshape(NB, TB),
        b.reshape(NB, TB),
        rows.reshape(1, TB),
        cols.reshape(1, TB),
        counts,
        rc.reshape(NB, TB),
        cc.reshape(NB, TB),
    )
    return -f.reshape(CELLS), -g.reshape(CELLS), gs * GROW, gt * GROW


def solution(mesh):
    placed = (
        P("row", None),
        P("col", None),
        P("row"),
        P("col"),
        P("row", "col", None),
        P("row", "col", None),
        P("row", "col"),
        P("row"),
        P("col"),
    )
    return jax.shard_map(
        on_device,
        mesh=mesh,
        in_specs=placed,
        out_specs=(P("row"), P("col"), P(("row", "col"), None), P(("col", "row"), None)),
        check_vma=False,
    )
```

```python
import jax
import jax.numpy as jnp
from jax import lax
from jax.experimental import pallas as pl
from jax.experimental.pallas import tpu as pltpu
from jax.sharding import PartitionSpec as P

MESH = pl.DeviceIdType.MESH
TB = 128
NB = 16
CELLS = NB * TB
E = 256
ROUNDS = 11
TALL = 8
HALF = TB // 2
SUBS = 2
SUB = E // SUBS
MASKED = -1e30
F32 = jnp.float32
BF16 = jnp.bfloat16
SHRINK = 2.0**-40
GROW = 2.0**40


def nt_dot(x, y):
    return lax.dot_general(x, y, (((1,), (1,)), ((), ())), preferred_element_type=F32)


def tn_dot(x, y):
    return lax.dot_general(x, y, (((0,), (0,)), ((), ())), preferred_element_type=F32)


def block(index, size=TB):
    return pl.ds(pl.multiple_of(index * size, size), size)


def kernel(
    src, tgt, a_ref, b_ref, rows_ref, cols_ref, count_ref, rc_ref, cc_ref,
    f_out, g_out, gs_out, gt_out,
    q, most, w, w_cols, part, land, wide, wide2, bias, vec, vec_w, srct, xs, ys, xb, yb, xt,
    gs_sum, gs_last, gs_land, gs_mid, gs_land2, gt_part, gt_sib, gt_sum, gt_land,
    ar_send, ar_recv, gs_ssem, gs_rsem, gs_ssem2, gs_rsem2, sib_ssem, sib_rsem, gt_ssem, gt_rsem,
):
    row_me = lax.axis_index("row")
    col_me = lax.axis_index("col")
    z_me = row_me // 2
    core = row_me % 2
    y_me = col_me // 4
    x_me = col_me % 4

    barrier = pltpu.get_barrier_semaphore()

    @pl.loop(1, NB)
    def _(k):
        pl.semaphore_signal(
            barrier, inc=1, device_id={"row": lax.rem(row_me + k, NB)}, device_id_type=MESH
        )
        pl.semaphore_signal(
            barrier, inc=1, device_id={"col": lax.rem(col_me + k, NB)}, device_id_type=MESH
        )

    eye = lax.broadcasted_iota(jnp.int32, (TB, TB), 0) == lax.broadcasted_iota(
        jnp.int32, (TB, TB), 1
    )

    def to_row(column):
        return jnp.sum(jnp.where(eye, column, 0.0), axis=0, keepdims=True)

    def to_column(row):
        return jnp.sum(jnp.where(eye, row, 0.0), axis=1, keepdims=True)

    def widen(value):
        vec[...] = value
        for rb in range(NB):
            wide[rb * TB : (rb + 1) * TB, :] = jnp.broadcast_to(
                to_column(vec[rb : rb + 1, :]), (TB, TB)
            )

    slot = lax.broadcasted_iota(jnp.int32, (TB, TB), 1)
    which = lax.broadcasted_iota(jnp.int32, (TB, TB), 0)
    live = slot < count_ref[...]
    row_hot = jnp.where((rows_ref[...] == which) & live, 1.0, 0.0).astype(BF16)
    col_hot = jnp.where((cols_ref[...] == which) & live, 1.0, 0.0).astype(BF16)
    present = nt_dot(row_hot[:NB], col_hot).astype(BF16)
    for cb in range(NB):
        spread = jnp.where(which == cb, 1.0, 0.0).astype(BF16)
        hits = jnp.dot(present, spread, preferred_element_type=F32)
        bias[:, cb * TB : (cb + 1) * TB] = jnp.where(hits > 0.5, 0.0, MASKED)

    @pl.loop(0, NB // TALL)
    def _(k):
        left = src[block(k, TALL * TB), :]
        for cb in range(NB // 2):
            at = slice(cb * 2 * TB, (cb + 1) * 2 * TB)
            s = nt_dot(left, tgt[at, :])
            for i in range(TALL):
                line = bias[pl.ds(k * TALL + i, 1), at]
                q[block(k * TALL + i), at] = s[i * TB : (i + 1) * TB] + line

    @pl.loop(0, NB)
    def _(rb):
        here = block(rb)
        top = q[here, 0:TB]
        for cb in range(1, NB):
            top = jnp.maximum(top, q[here, cb * TB : (cb + 1) * TB])
        total = jnp.exp(q[here, 0:TB] - top)
        for cb in range(1, NB):
            total += jnp.exp(q[here, cb * TB : (cb + 1) * TB] - top)
        wide[here, :] = top
        wide2[here, :] = total

    for rb in range(NB):
        here = slice(rb * TB, (rb + 1) * TB)
        top = wide[here, :]
        largest = jnp.max(top, axis=1, keepdims=True)
        total = jnp.sum(wide2[here, :] * jnp.exp(top - largest), axis=1, keepdims=True)
        part[0, rb : rb + 1, :] = to_row(largest + jnp.log(total))

    pl.semaphore_wait(barrier, 2 * (NB - 1))

    def start_reduce(index, axis):
        me = row_me if axis == "row" else col_me

        def send(k, carry):
            if axis == "row":
                j = k // 2
                far = lax.rem(4 + (1 - 2 * (j % 2)) * ((j + 1) // 2), 8)
                peer = lax.rem(z_me + far, 8) * 2 + lax.rem(core + 1 + k, 2)
            else:
                j = k // 4
                dy = lax.rem(2 + (1 - 2 * (j % 2)) * ((j + 1) // 2), 4)
                i = k % 4
                dx = lax.rem(2 + (1 - 2 * (i % 2)) * ((i + 1) // 2), 4)
                peer = lax.rem(y_me + dy, 4) * 4 + lax.rem(x_me + dx, 4)
            pltpu.make_async_remote_copy(
                src_ref=part.at[index],
                dst_ref=land.at[index, me],
                send_sem=ar_send.at[index],
                recv_sem=ar_recv.at[index],
                device_id={axis: peer},
                device_id_type=MESH,
            ).start()
            return carry

        lax.fori_loop(0, NB - 1, send, 0, unroll=True)
        land[index, me] = part[index]

    def end_reduce(index):
        others = land.at[index, pl.ds(0, NB - 1)]
        pltpu.make_async_copy(others, others, ar_recv.at[index]).wait()

    def summed(index):
        end_reduce(index)
        terms = [land[index, k] for k in range(NB)]
        while len(terms) > 1:
            terms = [terms[k] + terms[k + 1] for k in range(0, len(terms), 2)]
        return terms[0]

    def log_summed(index):
        end_reduce(index)
        largest = land[index, 0]
        for k in range(1, NB):
            largest = jnp.maximum(largest, land[index, k])
        total = jnp.exp(land[index, 0] - largest)
        for k in range(1, NB):
            total += jnp.exp(land[index, k] - largest)
        return largest + jnp.log(total)

    def row_pass(weights, index):
        vec_w[...] = weights

        @pl.loop(0, NB)
        def _(rb):
            here = block(rb)
            total = q[here, 0:TB] * vec_w[0:1, :]
            for cb in range(1, NB):
                total += q[here, cb * TB : (cb + 1) * TB] * vec_w[cb : cb + 1, :]
            wide[here, :] = total

        for rb in range(NB):
            total = jnp.sum(wide[rb * TB : (rb + 1) * TB, :], axis=1, keepdims=True)
            part[index, rb : rb + 1, :] = to_row(total)
        start_reduce(index, "col")

    def fold(value):
        total = value[0:8]
        for k in range(1, NB):
            total += value[k * 8 : (k + 1) * 8]
        return total

    def col_pass(weights, scale, index):
        widen(weights)

        def body(rb, totals):
            here = block(rb)
            u = wide[here, :]
            return tuple(
                totals[cb] + fold(q[here, cb * TB : (cb + 1) * TB] * u) for cb in range(NB)
            )

        totals = lax.fori_loop(0, NB, body, (jnp.zeros((8, TB), F32),) * NB)
        for cb in range(NB):
            vec[cb : cb + 1, :] = jnp.sum(totals[cb], axis=0, keepdims=True)
        part[index] = vec[...] * scale
        start_reduce(index, "row")

    start_reduce(0, "col")
    unit = jnp.where(
        lax.broadcasted_iota(jnp.int32, (E, E), 0) == lax.broadcasted_iota(jnp.int32, (E, E), 1),
        1.0,
        0.0,
    ).astype(BF16)
    for cb in range(NB // 2):
        at = slice(cb * 2 * TB, (cb + 1) * 2 * TB)
        srct[:, at] = nt_dot(unit, src[at, :]).astype(BF16)
    a = a_ref[...]
    b = b_ref[...]
    f1 = a - log_summed(0)

    widen(f1)

    def top_body(rb, tops):
        here = block(rb)
        u = wide[here, :]
        out = []
        for cb in range(NB):
            moved = q[here, cb * TB : (cb + 1) * TB] + u
            top = tops[cb]
            for k in range(NB):
                top = jnp.maximum(top, moved[k * 8 : (k + 1) * 8])
            out.append(top)
        return tuple(out)

    tops = lax.fori_loop(0, NB, top_body, (jnp.full((8, TB), MASKED, F32),) * NB)
    for cb in range(NB):
        vec_w[cb : cb + 1, :] = jnp.max(tops[cb], axis=0, keepdims=True)
    c = vec_w[...]

    def exp_body(rb, totals):
        here = block(rb)
        u = wide[here, :]
        out = []
        for cb in range(NB):
            at = slice(cb * TB, (cb + 1) * TB)
            value = jnp.exp((q[here, at] + u) - vec_w[cb : cb + 1, :])
            q[here, at] = value
            out.append(totals[cb] + fold(value))
        return tuple(out)

    totals = lax.fori_loop(0, NB, exp_body, (jnp.zeros((8, TB), F32),) * NB)
    for cb in range(NB):
        vec[cb : cb + 1, :] = jnp.sum(totals[cb], axis=0, keepdims=True)
    part[1] = c + jnp.log(vec[...])
    start_reduce(1, "row")
    exp_a = jnp.exp(a)
    exp_b = jnp.exp(b)
    inv_a = jnp.exp(-a)
    inv_b = jnp.exp(-b)
    g1 = b - log_summed(1)

    d = jnp.exp(c + g1)

    def put(ref, term, value):
        vec[...] = value
        for k in range(NB):
            ref[k * 8 + term : k * 8 + term + 1, :] = vec[k : k + 1, :]

    xs[...] = jnp.zeros_like(xs)
    ys[...] = jnp.zeros_like(ys)

    def thirds(value):
        first = value.astype(BF16).astype(F32)
        rest = value - first
        second = rest.astype(BF16).astype(F32)
        third = (rest - second).astype(BF16).astype(F32)
        return first, second, third

    def stacked(ref, to, order):
        for k in range(NB):
            parts = thirds(ref[k * 8 : (k + 1) * 8, :])
            to[:, k * TB : (k + 1) * TB] = jnp.concatenate(
                [parts[i] for i in order], axis=0
            ).astype(BF16)

    def stack_x():
        stacked(xs, xb, (0, 0, 1, 0, 2, 1))
        for k in range(NB // 2):
            at = slice(k * 2 * TB, (k + 1) * 2 * TB)
            xt[at, :] = nt_dot(unit, xb[:, at]).astype(BF16)

    def stack_y():
        stacked(ys, yb, (0, 1, 0, 2, 0, 1))

    def source_product(into, line, with_most):
        vec_w[...] = line

        @pl.loop(0, NB // TALL)
        def _(k):
            here = block(k, TALL * TB)
            for cb in range(NB):
                col = slice(cb * TB, (cb + 1) * TB)
                value = q[here, col] * vec_w[cb : cb + 1, :]
                if with_most:
                    value += most[here, col]
                w[:, col] = value.astype(BF16)
            into[here, :] = jnp.dot(w[...], tgt[...], preferred_element_type=F32)

    last_line = jnp.exp(c) * -SHRINK
    row_pass(d, 2)
    put(ys, 4, d * -SHRINK)
    u2 = exp_a / summed(2)
    col_pass(u2, d, 3)
    put(xs, 1, u2)
    source_product(gs_last, last_line, False)
    v2 = exp_b / summed(3)
    dv2 = d * v2
    row_pass(dv2, 4)
    put(ys, 3, dv2 * -SHRINK)
    u3 = exp_a / summed(4)
    col_pass(u3, d, 5)
    put(xs, 0, u3)
    f_out[...] = -(f1 + jnp.log(u3))
    v3 = exp_b / summed(5)

    y3 = d * v3 * inv_b * cc_ref[...]
    row_pass(y3, 6)
    put(ys, 0, y3 * -SHRINK)
    g_out[...] = -(g1 + jnp.log(v3))
    x3 = u3 * inv_a * (rc_ref[...] - u3 * summed(6))
    col_pass(x3, d, 7)
    put(xs, 3, x3)
    y2 = dv2 * inv_b * (-v2 * summed(7))
    row_pass(y2, 8)
    put(ys, 1, y2 * -SHRINK)
    x2 = u2 * inv_a * (-u2 * summed(8))
    col_pass(x2, d, 9)
    put(xs, 4, x2)
    stack_x()
    stack_y()

    @pl.loop(0, NB // TALL)
    def _(k):
        here = block(k, TALL * TB)
        for cb in range(NB // 2):
            at = slice(cb * 2 * TB, (cb + 1) * 2 * TB)
            factor = jnp.dot(xt[here, :], yb[:, at], preferred_element_type=F32)
            most[here, at] = q[here, at] * factor

    y1 = d * inv_b * -summed(9)
    row_pass(y1, 10)
    source_product(gs_sum, y1 * -SHRINK, True)
    x1 = inv_a * -summed(10)

    widen(x1)

    def first_copy(half, other, k):
        if half == 0:
            to_x = lax.rem(x_me + k, 4)
            owner, peer = other * 4 + to_x, y_me * 4 + to_x
        else:
            to_y = lax.rem(y_me + k, 4)
            owner, peer = to_y * 4 + other, to_y * 4 + x_me
        rows = pl.ds(pl.multiple_of(owner * TB + half * HALF, HALF), HALF)
        return pltpu.make_async_remote_copy(
            src_ref=gs_sum.at[rows],
            dst_ref=gs_land.at[half, other, x_me if half == 0 else y_me],
            send_sem=gs_ssem.at[half],
            recv_sem=gs_rsem.at[half, other],
            device_id={"col": peer},
            device_id_type=MESH,
        )

    def other_at(half, k):
        return lax.rem((y_me if half == 0 else x_me) + 2 + (1 - 2 * (k % 2)) * ((k + 1) // 2), 4)

    def second_stage(k):
        for half in range(2):
            other = other_at(half, k)
            others = gs_land.at[half, other, pl.ds(0, 3)]
            pltpu.make_async_copy(others, others, gs_rsem.at[half, other]).wait()
            mine = x_me if half == 0 else y_me
            owner = other * 4 + x_me if half == 0 else y_me * 4 + other
            rows = pl.ds(pl.multiple_of(owner * TB + half * HALF, HALF), HALF)
            total = gs_sum[rows, :]
            for far in range(1, 4):
                total += gs_land[half, other, lax.rem(mine + far, 4)]
            gs_mid[half, other] = total

            @pl.when(k < 3)
            def _():
                peer = other * 4 + x_me if half == 0 else y_me * 4 + other
                pltpu.make_async_remote_copy(
                    src_ref=gs_mid.at[half, other],
                    dst_ref=gs_land2.at[half, y_me if half == 0 else x_me],
                    send_sem=gs_ssem2.at[half],
                    recv_sem=gs_rsem2.at[half],
                    device_id={"col": peer},
                    device_id_type=MESH,
                ).start()

    def first_stage():
        @pl.loop(0, NB)
        def _(rb):
            here = block(rb)
            u = wide[here, :]
            for half in range(2):
                at = slice(half * TB, (half + 1) * TB)
                gs_sum[here, at] += u * gs_last[here, at]

        @pl.loop(0, 4)
        def _(k):
            for half in range(2):
                for far in (2, 1, 3):
                    first_copy(half, other_at(half, k), far).start()

    vec_w[...] = last_line
    vec[...] = y1 * -SHRINK

    def chip_at(k):
        return lax.rem(z_me + 4 + (1 - 2 * (k % 2)) * ((k + 1) // 2), 8)

    def sibling_copy(j):
        return pltpu.make_async_remote_copy(
            src_ref=gt_part.at[j, 1 - core],
            dst_ref=gt_sib.at[j],
            send_sem=sib_ssem.at[j],
            recv_sem=sib_rsem.at[j],
            device_id={"row": z_me * 2 + 1 - core},
            device_id_type=MESH,
        )

    def ring_copy(way, step, sub):
        j = lax.rem(z_me + jnp.where(way == 0, 4 - step, 4 + step), 8)
        rows = pl.ds(pl.multiple_of(sub * SUB, SUB), SUB)
        peer = lax.rem(z_me + jnp.where(way == 0, 1, 7), 8)
        return pltpu.make_async_remote_copy(
            src_ref=gt_sum.at[j, rows],
            dst_ref=gt_land.at[way, step, rows],
            send_sem=gt_ssem.at[way, step, sub],
            recv_sem=gt_rsem.at[way, step, sub],
            device_id={"row": peer * 2 + core},
            device_id_type=MESH,
        )

    def ready(k):
        j = chip_at(k)
        sibling_copy(j).wait_recv()
        gt_sum[j] = gt_part[j, core] + gt_sib[j]

    def advance(k):
        ready(k)
        j = chip_at(k)
        way = (k + 1) % 2
        step = (k + 1) // 2
        for i in range(SUBS):
            sub = (1 - way) * (1 - i) + way * i
            rows = pl.ds(pl.multiple_of(sub * SUB, SUB), SUB)

            @pl.when((step > 1) | (way == sub))
            def _():
                ring_copy(way, step - 1, sub).wait_recv()
                gt_sum[j, rows] += gt_land[way, step - 1, rows]

            ring_copy(way, step, sub).start()

    @pl.loop(0, 8)
    def _(k):
        j = chip_at(k)
        cols = block(j, 2 * TB)
        for part_k in range(NB // 2):
            here = slice(part_k * 2 * TB, (part_k + 1) * 2 * TB)
            u = wide[here, :]
            for half in range(2):
                col = block(j * 2 + half)
                last = vec_w[pl.ds(j * 2 + half, 1), :]
                line = vec[pl.ds(j * 2 + half, 1), :]
                value = most[here, col] + q[here, col] * (line + u * last)
                w_cols[here, half * TB : (half + 1) * TB] = value.astype(BF16)
        total = jnp.dot(srct[...], w_cols[...], preferred_element_type=F32)
        gt_part[j, 0] = total[:, :TB]
        gt_part[j, 1] = total[:, TB:]
        sibling_copy(j).start()

        @pl.when(k == 0)
        def _():
            first_stage()

        @pl.when(k == 1)
        def _():
            ready(0)
            for sub in range(SUBS):
                ring_copy(sub // (SUBS // 2), 0, sub).start()

        @pl.when(k > 1)
        def _():
            advance(k - 1)

        @pl.when(k > 4)
        def _():
            second_stage(k - 5)

    ready(7)
    second_stage(3)

    for way in range(2):
        for sub in range(SUBS):
            ring_copy(way, 3, sub).wait_recv()
    for k in range(2):
        at = slice(k * TB, (k + 1) * TB)
        total = gt_sum[z_me, at, :] + gt_land[0, 3, at, :] + gt_land[1, 3, at, :]
        gt_out[:, at] = total.T

    for half in range(2):
        others = gs_land2.at[half, pl.ds(0, 3)]
        pltpu.make_async_copy(others, others, gs_rsem2.at[half]).wait()
        mine = y_me if half == 0 else x_me
        total = gs_mid[half, mine]
        for far in range(1, 4):
            total += gs_land2[half, lax.rem(mine + far, 4)]
        gs_out[half * HALF : (half + 1) * HALF, :] = total

    @pl.loop(0, ROUNDS)
    def _(index):
        others = land.at[index, pl.ds(0, NB - 1)]
        pltpu.make_async_copy(others, others, ar_send.at[index]).wait()

    for half in range(2):
        others = gs_land.at[half, pl.ds(0, 3)]
        pltpu.make_async_copy(others, others, gs_ssem.at[half]).wait()
        others = gs_land2.at[half, pl.ds(0, 3)]
        pltpu.make_async_copy(others, others, gs_ssem2.at[half]).wait()

    @pl.loop(0, 8)
    def _(j):
        sibling_copy(j).wait_send()

    for sub in range(SUBS):
        ring_copy(sub // (SUBS // 2), 0, sub).wait_send()
        for way in range(2):
            for step in range(1, 4):
                ring_copy(way, step, sub).wait_send()


def on_device(src, tgt, a, b, rows, cols, counts, rc, cc):
    vmem = pl.BlockSpec(memory_space=pltpu.VMEM)
    dma = pltpu.SemaphoreType.DMA
    f, g, gs, gt = pl.pallas_call(
        kernel,
        out_shape=(
            jax.ShapeDtypeStruct((NB, TB), F32),
            jax.ShapeDtypeStruct((NB, TB), F32),
            jax.ShapeDtypeStruct((TB, E), F32),
            jax.ShapeDtypeStruct((TB, E), F32),
        ),
        in_specs=[vmem] * 9,
        out_specs=(vmem,) * 4,
        scratch_shapes=[
            pltpu.VMEM((CELLS, CELLS), F32),
            pltpu.VMEM((CELLS, CELLS), F32),
            pltpu.VMEM((TALL * TB, CELLS), BF16),
            pltpu.VMEM((CELLS, 2 * TB), BF16),
            pltpu.VMEM((ROUNDS, NB, TB), F32),
            pltpu.VMEM((ROUNDS, NB, NB, TB), F32),
            pltpu.VMEM((CELLS, TB), F32),
            pltpu.VMEM((CELLS, TB), F32),
            pltpu.VMEM((NB, CELLS), F32),
            pltpu.VMEM((NB, TB), F32),
            pltpu.VMEM((NB, TB), F32),
            pltpu.VMEM((E, CELLS), BF16),
            pltpu.VMEM((NB * 8, TB), F32),
            pltpu.VMEM((NB * 8, TB), F32),
            pltpu.VMEM((48, CELLS), BF16),
            pltpu.VMEM((48, CELLS), BF16),
            pltpu.VMEM((CELLS, 48), BF16),
            pltpu.VMEM((CELLS, E), F32),
            pltpu.VMEM((CELLS, E), F32),
            pltpu.VMEM((2, 4, 4, HALF, E), F32),
            pltpu.VMEM((2, 4, HALF, E), F32),
            pltpu.VMEM((2, 4, HALF, E), F32),
            pltpu.VMEM((8, 2, E, TB), F32),
            pltpu.VMEM((8, E, TB), F32),
            pltpu.VMEM((8, E, TB), F32),
            pltpu.VMEM((2, 4, E, TB), F32),
            dma((ROUNDS,)),
            dma((ROUNDS,)),
            dma((2,)),
            dma((2, 4)),
            dma((2,)),
            dma((2,)),
            dma((8,)),
            dma((8,)),
            dma((2, 4, SUBS)),
            dma((2, 4, SUBS)),
        ],
        compiler_params=pltpu.CompilerParams(
            collective_id=0, has_side_effects=True, vmem_limit_bytes=60 << 20
        ),
    )(
        src,
        tgt,
        a.reshape(NB, TB),
        b.reshape(NB, TB),
        rows.reshape(1, TB),
        cols.reshape(1, TB),
        counts,
        rc.reshape(NB, TB),
        cc.reshape(NB, TB),
    )
    return -f.reshape(CELLS), -g.reshape(CELLS), gs * GROW, gt * GROW


def solution(mesh):
    placed = (
        P("row", None),
        P("col", None),
        P("row"),
        P("col"),
        P("row", "col", None),
        P("row", "col", None),
        P("row", "col"),
        P("row"),
        P("col"),
    )
    return jax.shard_map(
        on_device,
        mesh=mesh,
        in_specs=placed,
        out_specs=(P("row"), P("col"), P(("row", "col"), None), P(("col", "row"), None)),
        check_vma=False,
    )
```
